512 devices in a mesh: rows: 128 (over y, z, core), cols: 4 (over x).
Axes of the slice: x: 4, y: 8, z: 8, core: 2. Of those that a mesh axis runs over, the one named last changes fastest.
Arguments:
- rhs: bfloat16 [98304, 512], P('rows', 'cols'), may hold values from -6 to 6
- left_butterfly: float32 [2, 2, 98304], P(None, None, 'rows'), may hold values from -4 to 4
- right_butterfly: float32 [2, 2, 98304], P(None, None, 'rows'), may hold values from -4 to 4
- pivots: float32 [98304], P('rows'), may hold values from -2 to 2, as said below
- panels: bfloat16 [2, 98304, 2048], P(None, ('rows', 'cols')), may hold values from -0.125 to 0.125
- inverse_blocks: bfloat16 [2, 2048, 2048], P(None, 'rows'), as said below
Outputs:
- solution: float32 [98304, 512], P('rows', 'cols')
The draws below stay inside these ranges and needn't reach their ends.
Inputs may be any that keep to these rules, and one draw needn't show every extreme that they name: `pivots`: magnitudes lie from 0.5 to 2, with either sign. `inverse_blocks`: each block is upper triangular with ones on its diagonal.
All inputs are finite; a program needn't handle non-finite values.
Results may differ from the reference program's by a relative error of at most 0.009.
Values may be sent and summed in bfloat16 or wider, within the bound.
No kernel may reach another device: no remote copies, remote signals or barrier semaphores. Data moves between devices by JAX's collectives and lax.ppermute only.
A program may use at most 64 MiB of HBM per device.

```python
import math
import jax
import jax.numpy as jnp
from jax import lax

NRHS = 512
BAND = 2048
RB = 16
CYC = 48
N = 98304
N_ROWS = 128


def draw_pivots(key, part):
    key = jax.random.fold_in(key, 11)
    sign_key, size_key = jax.random.split(key)
    signs = (2 * jax.random.randint(sign_key, (N,), 0, 2) - 1).astype(jnp.float32)
    sizes_drawn = jnp.exp(jax.random.uniform(size_key, (N,), jnp.float32, math.log(0.5), math.log(2.0)))
    return signs * sizes_drawn


def draw_inverse_blocks(key, part):
    key = jax.random.fold_in(key, 23)
    shape = (2, BAND, BAND)
    noise = jax.random.normal(key, shape, jnp.float32)
    row_ids = lax.broadcasted_iota(jnp.int32, shape, 1)
    col_ids = lax.broadcasted_iota(jnp.int32, shape, 2)
    upper = (col_ids > row_ids).astype(jnp.float32)
    unit = (col_ids == row_ids).astype(jnp.float32)
    return (noise * upper / math.sqrt(BAND) + unit).astype(jnp.bfloat16)


def steps_of(rng, dims, shards, smallest, largest):
    factor_of, own = 1.0, jax.random.fold_in(rng, 6)
    for position, shards_of in shards:
        steps = jnp.exp(jax.random.uniform(jax.random.fold_in(own, position), (shards_of,), jnp.float32, smallest / len(shards), largest / len(shards)))
        factor_of = factor_of * jnp.repeat(steps, dims[position] // shards_of).reshape([-1 if axis == position else 1 for axis in range(len(dims))])
    return factor_of


def gaussian(key, shape, spread, bound, pieces=(), held_as=jnp.bfloat16):
    drawn = jax.random.normal(key, shape, jnp.float32) * spread
    if len(pieces) > 0:
        drawn = steps_of(key, shape, pieces, -0.22, 0.18) * drawn
    return jnp.clip(drawn, min=-bound, max=bound).astype(held_as)


def setup_inputs(seed: int = 0) -> dict:
    splits = jax.random.split(jax.random.key(seed), 7)
    return {
        "rhs": gaussian(splits[0], (N, NRHS), 1.0, 6.0, ((0, 128), (1, 4))),
        "left_butterfly": gaussian(splits[1], (2, 2, N), 0.7, 4.0, ((2, 128),), jnp.float32),
        "right_butterfly": gaussian(splits[2], (2, 2, N), 0.7, 4.0, ((2, 128),), jnp.float32),
        "pivots": draw_pivots(jax.random.fold_in(splits[6], 71), 0),
        "panels": gaussian(splits[4], (2, N, BAND), BAND ** -0.5, 0.125, ((1, 512),)),
        "inverse_blocks": draw_inverse_blocks(jax.random.fold_in(splits[6], 71), 0),
    }


def outer_partner(values):
    half = values.shape[0] // 2
    return jnp.concatenate([values[half:], values[:half]], axis=0)


def inner_partner(values):
    quarter = values.shape[0] // 4
    shaped = values.reshape(2, 2, quarter, values.shape[1])
    return jnp.concatenate([shaped[:, 1:], shaped[:, :1]], axis=1).reshape(values.shape)


def apply_level(values, coef, partner, transposed):
    own_part = coef[0][:, None]
    cross = coef[1][:, None]
    if transposed:
        return own_part * values + partner(cross * values)
    return own_part * values + cross * partner(values)


def reference(rhs, left_butterfly, right_butterfly, pivots, panels, inverse_blocks):
    contract = (((0,), (0,)), ((), ()))
    work = rhs.astype(jnp.float32)
    work = apply_level(work, left_butterfly[0], outer_partner, True)
    work = apply_level(work, left_butterfly[1], inner_partner, True)
    work = work.reshape(N_ROWS, CYC, RB, NRHS)
    for band_index in range(2):
        band_in = work[:, band_index].reshape(BAND, NRHS).astype(jnp.bfloat16)
        solved = lax.dot_general(inverse_blocks[band_index], band_in, contract, preferred_element_type=jnp.float32)
        work = work.at[:, band_index].set(solved.reshape(N_ROWS, RB, NRHS))
        rounded = solved.astype(jnp.bfloat16)
        lower = panels[band_index].reshape(N_ROWS, CYC, RB, BAND)[:, band_index + 1:].reshape(-1, BAND)
        update = jnp.dot(lower, rounded, preferred_element_type=jnp.float32)
        update = update.reshape(N_ROWS, CYC - band_index - 1, RB, NRHS)
        work = work.at[:, band_index + 1:].set(work[:, band_index + 1:] - update)
    scaled = work / pivots.reshape(N_ROWS, CYC, RB, 1)
    result = scaled
    for band_index in (1, 0):
        lower = panels[band_index].reshape(N_ROWS, CYC, RB, BAND)[:, band_index + 1:].reshape(-1, BAND)
        below = result[:, band_index + 1:].reshape(-1, NRHS).astype(jnp.bfloat16)
        term = lax.dot_general(lower, below, contract, preferred_element_type=jnp.float32)
        target = scaled[:, band_index].reshape(BAND, NRHS) - term
        solved = jnp.dot(inverse_blocks[band_index], target.astype(jnp.bfloat16), preferred_element_type=jnp.float32)
        result = result.at[:, band_index].set(solved.reshape(N_ROWS, RB, NRHS))
    flat = result.reshape(N, NRHS)
    flat = apply_level(flat, right_butterfly[1], inner_partner, False)
    flat = apply_level(flat, right_butterfly[0], outer_partner, False)
    return flat
```

```python
import jax
import jax.numpy as jnp
import numpy as np
from jax import lax
from jax.sharding import Mesh, PartitionSpec as P

BF = jnp.bfloat16
F32 = jnp.float32
ROWS = ("y", "z", "c")
T0 = (((0,), (0,)), ((), ()))


def grid_of(rows):
    z = 8 if rows >= 128 else 2
    return rows // (2 * z), z, 2


def swap_y(v, bit, count):
    return lax.ppermute(v, "y", [(i, i ^ bit) for i in range(count)])


def swap_core(v):
    return lax.ppermute(v, "c", [(0, 1), (1, 0)])


def everyone(block, axes, count):
    return lax.all_to_all(jnp.broadcast_to(block[None], (count,) + block.shape), axes, 0, 0)


def two_parts(v):
    high = v.astype(BF)
    return high, (v - high.astype(F32)).astype(BF)


def total(v):
    return jnp.sum(v.astype(F32), axis=0)


def shards(rhs, left, right, pivots, panels, inverse):
    ny, nz, nx = lax.axis_size("y"), lax.axis_size("z"), lax.axis_size("x")
    nzc = 2 * nz
    rb, band = inverse.shape[1], inverse.shape[2]
    width = rhs.shape[1]
    yb = nzc * rb
    low, core = 2 * rb, lax.axis_index("c")
    outer, inner = ny // 2, ny // 4
    first_core = core == 0

    def gather_all(block):
        mine = everyone(block, ("y", "z"), ny * nz)
        other = swap_core(mine)
        even = jnp.where(first_core, mine, other)
        odd = jnp.where(first_core, other, mine)
        return jnp.stack([even, odd], axis=1).reshape(band, width)

    def reduce_all(part):
        part = part.reshape(ny * nz, 2, rb, width)
        away = jnp.where(first_core, part[:, 1], part[:, 0]).astype(BF)
        mine = jnp.where(first_core, part[:, 0], part[:, 1])
        mine = (mine + swap_core(away).astype(F32)).astype(BF)
        return total(lax.all_to_all(mine, ("y", "z"), 0, 0))

    def reduce_zc(part):
        return total(lax.all_to_all(part.astype(BF).reshape(nzc, rb, width), ("z", "c"), 0, 0))

    cross_rows = lax.all_gather(panels[0, rb:low], ("y", "x"), axis=0, tiled=False)
    cross_rows = cross_rows.reshape(ny, nx, rb, band)[:, 0].reshape(ny * rb, band)
    gathered = lax.all_gather(panels, "x", axis=1, tiled=True)

    def columns(coef):
        v = coef[:, :, :low].reshape(8, rb).T
        return jnp.concatenate(two_parts(v), axis=1)

    table = jnp.concatenate([columns(left), columns(right)], axis=1)
    table = jnp.pad(table, ((0, 0), (0, yb - table.shape[1])))
    raw = jnp.concatenate([rhs[:rb], rhs[rb:low]], axis=1)
    if raw.shape[1] < yb:
        raw = jnp.pad(raw, ((0, 0), (0, yb - raw.shape[1])))
    tiles = inverse.reshape(2, rb, ny, yb).transpose(2, 0, 1, 3)
    shared = jnp.broadcast_to(jnp.stack([raw, table])[None], (ny, 2, rb, yb))
    message = jnp.concatenate([tiles, shared], axis=1)
    arrived = lax.all_to_all(message, "y", 0, 0)
    tile0 = arrived[:, 0].reshape(ny * rb, yb)
    tile1 = arrived[:, 1].reshape(ny * rb, yb)
    raws = arrived[:, 2].astype(F32)
    table = arrived[:, 3].astype(F32)

    def coefs(offset):
        v = table[:, :, offset:offset + 8] + table[:, :, offset + 8:offset + 16]
        return lambda level, which, b: v[:, :, level * 4 + which * 2 + b, None]

    lc, rc = coefs(0), coefs(16)
    pair = lambda v, bit: jnp.concatenate(
        [v[i ^ bit][None] for i in range(ny)], axis=0)

    def rotated(b):
        v = raws[:, :, b * width:(b + 1) * width]
        v = lc(0, 0, b) * v + pair(lc(0, 1, b) * v, outer)
        v = lc(1, 0, b) * v + pair(lc(1, 1, b) * v, inner)
        return v.reshape(ny * rb, width)

    x0, x1 = rotated(0), rotated(1)

    below = rhs[low:].astype(F32)
    c = left[:, :, low:, None]
    below = c[0, 0] * below + swap_y((c[0, 1] * below).astype(BF), outer, ny).astype(F32)
    below = c[1, 0] * below + swap_y((c[1, 1] * below).astype(BF), inner, ny).astype(F32)

    own0 = reduce_zc(lax.dot_general(tile0, x0.astype(BF), T0, preferred_element_type=F32))
    s0 = gather_all(own0.astype(BF))
    x1 = x1 - jnp.dot(cross_rows, s0, preferred_element_type=F32)
    own1 = reduce_zc(lax.dot_general(tile1, x1.astype(BF), T0, preferred_element_type=F32))
    s1 = gather_all(own1.astype(BF))
    s0, s1 = lax.optimization_barrier((s0, s1))

    update = jnp.dot(gathered[0], s0, preferred_element_type=F32)
    update += jnp.dot(gathered[1], s1, preferred_element_type=F32)
    scaled = (below - update[low:]) / pivots[low:, None]
    rounded = scaled.astype(BF)
    padded = jnp.concatenate([jnp.zeros((low, width), BF), rounded], axis=0)
    term1 = lax.dot_general(gathered[1], padded, T0, preferred_element_type=F32)
    term0 = lax.dot_general(gathered[0], padded, T0, preferred_element_type=F32)

    d = right[:, :, low:, None]
    out = d[1, 0] * scaled + d[1, 1] * swap_y(rounded, inner, ny).astype(F32)
    out = d[0, 0] * out + d[0, 1] * swap_y(out.astype(BF), outer, ny).astype(F32)

    target1 = own1 / pivots[rb:low, None] - reduce_all(term1)
    t1 = everyone(target1.astype(BF), ("z", "c"), nzc).reshape(yb, width)
    back1 = jnp.dot(tile1, t1, preferred_element_type=F32)
    term0 += lax.dot_general(cross_rows, back1.astype(BF), T0, preferred_element_type=F32)
    target0 = own0 / pivots[:rb, None] - reduce_all(term0)
    t0 = everyone(target0.astype(BF), ("z", "c"), nzc).reshape(yb, width)
    back0 = jnp.dot(tile0, t0, preferred_element_type=F32)

    def finished(v, b):
        v = v.reshape(ny, rb, width)
        v = rc(1, 0, b) * v + rc(1, 1, b) * pair(v, inner)
        return rc(0, 0, b) * v + rc(0, 1, b) * pair(v, outer)

    last = jnp.concatenate([finished(back0, 0), finished(back1, 1)], axis=1).astype(BF)
    head = total(lax.all_to_all(last, "y", 0, 0))
    return jnp.concatenate([head, out], axis=0)


def solution(mesh):
    rows, cols = mesh.devices.shape
    grid = Mesh(mesh.devices.reshape(grid_of(rows) + (cols,)), ("y", "z", "c", "x"))
    in_specs = (
        P(ROWS, "x"),
        P(None, None, ROWS),
        P(None, None, ROWS),
        P(ROWS),
        P(None, ROWS + ("x",), None),
        P(None, ROWS, None),
    )
    return jax.shard_map(
        shards, mesh=grid, in_specs=in_specs, out_specs=P(ROWS, "x"), check_vma=False)
```

```python
import jax
import jax.numpy as jnp
from jax import lax
from jax.experimental import pallas as pl
from jax.experimental.pallas import tpu as pltpu
from jax.sharding import Mesh, PartitionSpec as P

BF = jnp.bfloat16
F32 = jnp.float32
ROWS = ("y", "z", "c")
DOWN = (((0,), (0,)), ((), ()))


def grid_of(rows):
    z = 8 if rows >= 128 else 4
    return rows // (2 * z), z, 2


def swap_y(v, bit, count):
    return lax.ppermute(v, "y", [(i, i ^ bit) for i in range(count)])


def swap_core(v):
    return lax.ppermute(v, "c", [(0, 1), (1, 0)])


def everyone(block, axes, count):
    return lax.all_to_all(jnp.broadcast_to(block[None], (count,) + block.shape), axes, 0, 0)


def two_parts(v):
    high = v.astype(BF)
    return high, (v - high.astype(F32)).astype(BF)


def total(v):
    return jnp.sum(v.astype(F32), axis=0)


def dot(a, b):
    return jnp.dot(a, b, preferred_element_type=F32)


def down(a, b):
    return lax.dot_general(a, b, DOWN, preferred_element_type=F32)


LO, LI, RO, RI, PIV = 0, 2, 4, 6, 8


def column(table, k):
    return table[:, k:k + 1]


def elementwise(body, outs, *args):
    size = sum(a.size * a.dtype.itemsize for a in args)
    return pl.pallas_call(
        body,
        out_shape=outs,
        cost_estimate=pl.CostEstimate(flops=0, bytes_accessed=2 * size, transcendentals=0),
    )(*args)


def left_send(rhs, table, send):
    send[...] = (column(table, LO + 1) * rhs[...].astype(F32)).astype(BF)


def left_middle(rhs, got, table, value, send):
    v = column(table, LO) * rhs[...].astype(F32) + got[...].astype(F32)
    value[...] = column(table, LI) * v
    send[...] = (column(table, LI + 1) * v).astype(BF)


def right_middle(scaled, got, table, value, send):
    v = column(table, RI) * scaled[...] + column(table, RI + 1) * got[...].astype(F32)
    value[...] = column(table, RO) * v
    send[...] = v.astype(BF)


def right_end(value, got, table, out):
    out[...] = value[...] + column(table, RO + 1) * got[...].astype(F32)


def first_update(panel, solved, value, got, base):
    base[...] = value[...] + got[...].astype(F32) - dot(panel[...], solved[...])


def split_term(core, acc, mine, away):
    ny, half, width = mine.shape
    for y in range(ny):
        for h in range(2):
            start = (2 * y + h) * half
            block = acc[:, start:start + half].T

            @pl.when(core[0] == h)
            def _():
                mine[y] = block

            @pl.when(core[0] != h)
            def _():
                away[y] = block.astype(BF)


def middle(low, tile, core, panel, solved, base, table, scaled, rounded, mine, away, acc):
    step = pl.program_id(0)
    v = (base[...] - dot(panel[...], solved[...])) / column(table, PIV)
    scaled[...] = v
    row = lax.broadcasted_iota(jnp.int32, v.shape, 0) + step * tile
    kept = jnp.where(row >= low, v, 0.0)
    rounded[...] = kept.astype(BF)
    add = dot(kept.T.astype(BF), panel[...])

    @pl.when(step == 0)
    def _():
        acc[...] = add

    @pl.when(step > 0)
    def _():
        acc[...] += add

    @pl.when(step == pl.num_programs(0) - 1)
    def _():
        split_term(core, acc, mine, away)


def first_term(core, panel, rounded, mine, away, acc):
    step = pl.program_id(0)
    add = dot(rounded[...].astype(F32).T.astype(BF), panel[...])

    @pl.when(step == 0)
    def _():
        acc[...] = add

    @pl.when(step > 0)
    def _():
        acc[...] += add

    @pl.when(step == pl.num_programs(0) - 1)
    def _():
        split_term(core, acc, mine, away)


def start_bands(ny, outer, inner, coefs, arrived, part, x1):
    rb, width = arrived.shape[2:]
    n = 2 * ny

    def fly(b, i, level, v):
        bit = (outer if level == 0 else inner) * 2
        own = level * 4 + b
        j = i ^ bit
        a = coefs[i][:, own:own + 1] * v[i]
        return a + coefs[j][:, own + 2:own + 3] * v[j]

    both = []
    for b in range(2):
        raw = [arrived[i, 3 + b].astype(F32) for i in range(n)]
        first = [fly(b, i, 0, raw) for i in range(n)]
        both.append([fly(b, i, 1, first) for i in range(n)])
    tile = jnp.concatenate([arrived[i, 0] for i in range(n)], axis=0)
    x0 = jnp.concatenate(both[0], axis=0).astype(BF)
    part[...] = down(tile, x0).astype(BF)
    for i in range(n):
        x1[i] = both[1][i]


def shards(rhs, left, right, pivots, panels, inverse):
    ny, nz = lax.axis_size("y"), lax.axis_size("z")
    rb, band = inverse.shape[1], inverse.shape[2]
    rows, width = rhs.shape
    half = nz * rb
    low = 2 * rb
    core, y, z = lax.axis_index("c"), lax.axis_index("y"), lax.axis_index("z")
    outer, inner = ny // 2, ny // 4
    chunk = ny * 2 * rb
    first_core = core == 0
    once = jnp.where(first_core, 1.0, 0.0).astype(F32)
    core_ref = core.astype(jnp.int32)[None]

    def both_halves(mine):
        other = swap_core(mine)
        even = jnp.where(first_core, mine, other)
        odd = jnp.where(first_core, other, mine)
        return jnp.stack([even, odd], axis=1).reshape(band, width)

    def reduce_y_everywhere_z(mine):
        v = total(lax.all_to_all(mine.astype(BF), "y", 0, 0))
        return total(everyone(v.astype(BF), "z", nz))

    gathered0 = lax.all_gather(panels[0], "x", axis=0, tiled=True)
    gathered1 = lax.all_gather(panels[1], "x", axis=0, tiled=True)

    table = jnp.concatenate([left.reshape(4, rows), right.reshape(4, rows), pivots[None]], axis=0)
    table = jnp.pad(table, ((0, 7), (0, 0))).T

    few = table[:low].reshape(2, rb, 16).transpose(1, 2, 0).reshape(rb, 32)
    few = jnp.concatenate(two_parts(few), axis=1)
    few = jnp.pad(few, ((0, 0), (0, half - few.shape[1])))
    blocks = inverse.reshape(2, rb, ny, 2, half)
    wide0 = blocks[0].transpose(1, 2, 0, 3)[:, :, None]
    wide1 = jnp.broadcast_to(blocks[1].transpose(1, 2, 0, 3)[:, None], (ny, 2, 2, rb, half))
    shared = jnp.concatenate([rhs[:low].reshape(2, rb, half), few[None]], axis=0)
    shared = jnp.broadcast_to(shared[None, None], (ny, 2, 3, rb, half))
    message = jnp.concatenate([wide0, wide1, shared], axis=2).reshape(ny * 2, 6, rb, half)
    arrived = lax.all_to_all(message, ("y", "c"), 0, 0)

    shape = jax.ShapeDtypeStruct
    whole, sent = shape((rows, width), F32), shape((rows, width), BF)
    send = elementwise(left_send, sent, rhs, table)
    value, send = elementwise(
        left_middle, (whole, sent), rhs, swap_y(send, outer, ny), table)
    crossed = swap_y(send, inner, ny)

    small = arrived[:, 5].astype(F32)
    small = small[:, :, :32] + small[:, :, 32:64]
    tile0 = arrived[:, 0].reshape(chunk, half)
    tile1 = jnp.concatenate(
        [arrived[:, 1].reshape(chunk, half), arrived[:, 2].reshape(chunk, half)], axis=1)

    part, x1 = pl.pallas_call(
        lambda *refs: start_bands(ny, outer, inner, *refs),
        out_shape=(shape((half, width), BF), shape((ny * 2, rb, width), F32)),
    )(small, arrived)
    x1 = once * lax.dynamic_slice_in_dim(x1, 2 * y, 2, 0).reshape(low, width)

    few = lax.dynamic_slice_in_dim(arrived[:, 5], 2 * y, 2, 0)
    few = jnp.concatenate(
        [few[c, :, o + 2 * PIV:o + 2 * PIV + 2] for c in (0, 1) for o in (0, 32)], axis=1)
    few = jnp.pad(few, ((0, 0), (0, width - few.shape[1])))
    met = everyone(jnp.concatenate([part, few], axis=0), "z", nz)
    half0 = total(met[:, :half])
    few = lax.dynamic_slice_in_dim(met[:, half:], core * (nz // 2), nz // 2, 0).astype(F32)
    own_pivots = [
        jnp.stack([few[:, :, 4 * c + b] + few[:, :, 4 * c + 2 + b] for c in (0, 1)], axis=1)
        .reshape(half, 1) for b in (0, 1)]
    mine0 = everyone(half0.astype(BF), "y", ny)
    s0 = both_halves(mine0)

    cross = gathered0[rb:low].reshape(rb, ny, 2, half)
    cross_mine = jnp.where(first_core, cross[:, :, 0], cross[:, :, 1]).reshape(rb, ny * half)
    cross_away = jnp.where(first_core, cross[:, :, 1], cross[:, :, 0]).reshape(rb, ny * half)
    cross_got = swap_core(cross_away)
    cross = jnp.concatenate([
        jnp.where(first_core, cross_mine, cross_got),
        jnp.where(first_core, cross_got, cross_mine)], axis=0)
    x1 = x1 - dot(cross, mine0.reshape(ny * half, width))
    x1 = everyone(x1.astype(BF), "y", ny).reshape(chunk, width)
    part = down(tile1, x1).reshape(2, half, width)
    away = swap_core(jnp.where(first_core, part[1], part[0]).astype(BF)).astype(F32)
    part = jnp.where(first_core, part[0], part[1]) + away
    half1 = total(everyone(part.astype(BF), "z", nz))

    tile = rows // 3
    steps = rows // tile
    panel_spec = pl.BlockSpec((tile, band), lambda i: (i, 0))
    solved_spec = pl.BlockSpec((band, width), lambda i: (0, 0))
    row_spec = pl.BlockSpec((tile, width), lambda i: (i, 0))
    table_spec = pl.BlockSpec((tile, 16), lambda i: (i, 0))
    core_spec = pl.BlockSpec(memory_space=pltpu.SMEM)
    half_spec = pl.BlockSpec((ny, half, width), lambda i: (0, 0, 0))
    params = pltpu.CompilerParams(vmem_limit_bytes=40 * 2 ** 20)
    cost = pl.CostEstimate(
        flops=2 * rows * band * width, bytes_accessed=2 * rows * band, transcendentals=0)
    base = pl.pallas_call(
        first_update, out_shape=whole, grid=(steps,),
        in_specs=[panel_spec, solved_spec, row_spec, row_spec], out_specs=row_spec,
        compiler_params=params, cost_estimate=cost,
    )(gathered0, s0, value, crossed)

    s1 = both_halves(everyone(half1.astype(BF), "y", ny))
    halves = (shape((ny, half, width), F32), shape((ny, half, width), BF))
    scaled, rounded, mine1, away1 = pl.pallas_call(
        lambda *refs: middle(low, tile, *refs),
        out_shape=(whole, sent) + halves, grid=(steps,),
        in_specs=[core_spec, panel_spec, solved_spec, row_spec, table_spec],
        out_specs=(row_spec, row_spec, half_spec, half_spec),
        scratch_shapes=[pltpu.VMEM((width, band), F32)],
        compiler_params=params, cost_estimate=cost,
    )(core_ref, gathered1, s1, base, table)
    target1 = half1 / own_pivots[1] - reduce_y_everywhere_z(
        mine1 + swap_core(away1).astype(F32))

    mine0, away0 = pl.pallas_call(
        first_term, out_shape=halves, grid=(steps,),
        in_specs=[core_spec, panel_spec, row_spec], out_specs=(half_spec, half_spec),
        scratch_shapes=[pltpu.VMEM((width, band), F32)],
        compiler_params=params, cost_estimate=cost,
    )(core_ref, gathered0, rounded)
    mine0 = mine0 + swap_core(away0).astype(F32)

    value, send = elementwise(
        right_middle, (whole, sent), scaled, swap_y(rounded, inner, ny), table)
    out = elementwise(right_end, whole, value, swap_y(send, outer, ny), table)

    t1 = target1.astype(BF)
    other = swap_core(t1)
    t1 = jnp.concatenate([
        jnp.where(first_core, t1, other), jnp.where(first_core, other, t1)], axis=0)
    back1 = dot(tile1, t1)
    solved1 = total(lax.all_to_all(back1.astype(BF).reshape(ny, low, width), "y", 0, 0))
    mine0 = mine0 + down(cross, solved1.astype(BF)).reshape(ny, half, width)
    target0 = half0 / own_pivots[0] - reduce_y_everywhere_z(mine0)
    back0 = dot(tile0, target0.astype(BF))

    def pair(v, bit):
        return jnp.concatenate([v[i ^ bit][None] for i in range(ny)], axis=0)

    def finished(v, b):
        v = v.reshape(ny, 2, rb, width)
        k = small.reshape(ny, 2, rb, 32)
        at = lambda column: k[:, :, :, 2 * column + b, None]
        v = at(RI) * v + at(RI + 1) * pair(v, inner)
        return at(RO) * v + at(RO + 1) * pair(v, outer)

    last = jnp.stack([finished(back0, 0), finished(once * back1, 1)], axis=2)
    last = last.astype(BF).reshape(ny * 2, low, width)
    head = total(lax.all_to_all(last, ("y", "c"), 0, 0))
    return lax.dynamic_update_slice(out, head, (0, 0))


def solution(mesh):
    rows, cols = mesh.devices.shape
    grid = Mesh(mesh.devices.reshape(grid_of(rows) + (cols,)), ("y", "z", "c", "x"))
    in_specs = (
        P(ROWS, "x"),
        P(None, None, ROWS),
        P(None, None, ROWS),
        P(ROWS),
        P(None, ROWS + ("x",), None),
        P(None, ROWS, None),
    )
    return jax.shard_map(
        shards, mesh=grid, in_specs=in_specs, out_specs=P(ROWS, "x"), check_vma=False)
```

```python
import jax
import jax.numpy as jnp
from jax import lax
from jax.experimental import pallas as pl
from jax.experimental.pallas import tpu as pltpu
from jax.sharding import Mesh, PartitionSpec as P

BF = jnp.bfloat16
F32 = jnp.float32
ROWS = ("y", "z", "c")
DOWN = (((0,), (0,)), ((), ()))


def grid_of(rows):
    z = 8 if rows >= 128 else 4
    return rows // (2 * z), z, 2


def swap_y(v, bit, count):
    return lax.ppermute(v, "y", [(i, i ^ bit) for i in range(count)])


def swap_core(v):
    return lax.ppermute(v, "c", [(0, 1), (1, 0)])


def everyone(block, axes, count):
    return lax.all_to_all(jnp.broadcast_to(block[None], (count,) + block.shape), axes, 0, 0)


def two_parts(v):
    high = v.astype(BF)
    return high, (v - high.astype(F32)).astype(BF)


def total(v):
    return jnp.sum(v.astype(F32), axis=0)


def dot(a, b):
    return jnp.dot(a, b, preferred_element_type=F32)


def down(a, b):
    return lax.dot_general(a, b, DOWN, preferred_element_type=F32)


LO, LI, RO, RI, PIV = 0, 2, 4, 6, 8


def column(table, k):
    return table[:, k:k + 1]


def elementwise(body, outs, *args):
    size = sum(a.size * a.dtype.itemsize for a in args)
    return pl.pallas_call(
        body,
        out_shape=outs,
        cost_estimate=pl.CostEstimate(flops=0, bytes_accessed=2 * size, transcendentals=0),
    )(*args)


def left_send(rhs, table, send):
    send[...] = (column(table, LO + 1) * rhs[...].astype(F32)).astype(BF)


def left_middle(rhs, got, table, value, send):
    v = column(table, LO) * rhs[...].astype(F32) + got[...].astype(F32)
    value[...] = column(table, LI) * v
    send[...] = (column(table, LI + 1) * v).astype(BF)


def right_middle(scaled, got, table, value, send):
    v = column(table, RI) * scaled[...] + column(table, RI + 1) * got[...].astype(F32)
    value[...] = column(table, RO) * v
    send[...] = v.astype(BF)


def right_end(value, got, table, out):
    out[...] = value[...] + column(table, RO + 1) * got[...].astype(F32)


def assemble(core, mine, other, solved):
    ny, half, _ = mine.shape
    for y in range(ny):
        for h in range(2):
            start = (2 * y + h) * half

            @pl.when(core[0] == h)
            def _():
                solved[start:start + half] = mine[y]

            @pl.when(core[0] != h)
            def _():
                solved[start:start + half] = other[y]


def first_update(core, panel, mine, other, value, got, base, solved):
    @pl.when(pl.program_id(0) == 0)
    def _():
        assemble(core, mine, other, solved)

    base[...] = value[...] + got[...].astype(F32) - dot(panel[...], solved[...])


def split_term(core, acc, mine, away):
    ny, half, width = mine.shape
    for y in range(ny):
        for h in range(2):
            start = (2 * y + h) * half
            block = acc[:, start:start + half].T

            @pl.when(core[0] == h)
            def _():
                mine[y] = block

            @pl.when(core[0] != h)
            def _():
                away[y] = block.astype(BF)


def middle(
        low, tile, core, panel, own, other, base, table, scaled, rounded, mine, away, acc, solved):
    step = pl.program_id(0)

    @pl.when(step == 0)
    def _():
        assemble(core, own, other, solved)

    v = (base[...] - dot(panel[...], solved[...])) / column(table, PIV)
    scaled[...] = v
    row = lax.broadcasted_iota(jnp.int32, v.shape, 0) + step * tile
    kept = jnp.where(row >= low, v, 0.0)
    rounded[...] = kept.astype(BF)
    add = dot(kept.T.astype(BF), panel[...])

    @pl.when(step == 0)
    def _():
        acc[...] = add

    @pl.when(step > 0)
    def _():
        acc[...] += add

    @pl.when(step == pl.num_programs(0) - 1)
    def _():
        split_term(core, acc, mine, away)


def first_term(core, panel, rounded, mine, away, acc):
    step = pl.program_id(0)
    add = dot(rounded[...].astype(F32).T.astype(BF), panel[...])

    @pl.when(step == 0)
    def _():
        acc[...] = add

    @pl.when(step > 0)
    def _():
        acc[...] += add

    @pl.when(step == pl.num_programs(0) - 1)
    def _():
        split_term(core, acc, mine, away)


def second_input(core, x1, mine_rows, other_rows, solved, spread, rows):
    ny, half, width = solved.shape
    rb = mine_rows.shape[0]
    first = jnp.where(core[0] == 0, 1.0, 0.0)

    @pl.when(core[0] == 0)
    def _():
        rows[:rb] = mine_rows[...]
        rows[rb:] = other_rows[...]

    @pl.when(core[0] != 0)
    def _():
        rows[:rb] = other_rows[...]
        rows[rb:] = mine_rows[...]

    v = first * x1[...]
    for y in range(ny):
        start = pl.multiple_of((2 * y + core[0]) * half, half)
        v = v - dot(rows[:, pl.ds(start, half)], solved[y])
    v = v.astype(BF)
    for y in range(ny):
        spread[y] = v


def cross_back(core, tile, target, cross, term, away, back, out):
    ny, half, _ = term.shape
    v = dot(tile[...], target[...])
    back[...] = v
    turned = v.T.astype(BF)
    for y in range(ny):
        start = pl.multiple_of((2 * y + core[0]) * half, half)
        share = dot(turned, cross[:, pl.ds(start, half)]).T
        out[y] = (term[y] + away[y].astype(F32) + share).astype(BF)


def end_bands(ny, outer, inner, core, coefs, tile, target, back1, last):
    n, rb = coefs.shape[:2]
    first = jnp.where(core[0] == 0, 1.0, 0.0)
    values = [dot(tile[...], target[...]), first * back1[...]]
    for b in range(2):
        v = [values[b][i * rb:(i + 1) * rb] for i in range(n)]
        for level, bit in ((RI, 2 * inner), (RO, 2 * outer)):
            k = 2 * level + b
            v = [coefs[i][:, k:k + 1] * v[i] + coefs[i][:, k + 2:k + 3] * v[i ^ bit]
                 for i in range(n)]
        for i in range(n):
            last[i, b * rb:(b + 1) * rb] = v[i].astype(BF)


def spread_sum(arrived, count, base=None, pivots=None):
    rb, width = arrived.shape[1:]

    def body(*refs):
        own, spread = refs[-2:]
        v = jnp.sum(refs[0][...].astype(F32), axis=0)
        if base is not None:
            v = refs[1][...] / refs[2][...] - v
        own[...] = v
        v = v.astype(BF)
        for i in range(count):
            spread[i] = v

    args = (arrived,) if base is None else (arrived, base, pivots)
    return pl.pallas_call(
        body,
        out_shape=(jax.ShapeDtypeStruct((rb, width), F32),
                   jax.ShapeDtypeStruct((count, rb, width), BF)),
        cost_estimate=pl.CostEstimate(
            flops=0, bytes_accessed=2 * arrived.size, transcendentals=0),
    )(*args)


def start_bands(ny, outer, inner, coefs, arrived, part, x1):
    rb, width = arrived.shape[2:]
    n = 2 * ny

    def fly(b, i, level, v):
        bit = (outer if level == 0 else inner) * 2
        own = level * 4 + b
        j = i ^ bit
        a = coefs[i][:, own:own + 1] * v[i]
        return a + coefs[j][:, own + 2:own + 3] * v[j]

    both = []
    for b in range(2):
        raw = [arrived[i, 3 + b].astype(F32) for i in range(n)]
        first = [fly(b, i, 0, raw) for i in range(n)]
        both.append([fly(b, i, 1, first) for i in range(n)])
    tile = jnp.concatenate([arrived[i, 0] for i in range(n)], axis=0)
    x0 = jnp.concatenate(both[0], axis=0).astype(BF)
    part[...] = down(tile, x0).astype(BF)
    for i in range(n):
        x1[i] = both[1][i]


def shards(rhs, left, right, pivots, panels, inverse):
    ny, nz = lax.axis_size("y"), lax.axis_size("z")
    rb, band = inverse.shape[1], inverse.shape[2]
    rows, width = rhs.shape
    half = nz * rb
    low = 2 * rb
    core, y = lax.axis_index("c"), lax.axis_index("y")
    outer, inner = ny // 2, ny // 4
    chunk = ny * 2 * rb
    core_ref = core.astype(jnp.int32)[None]

    def reduce_yz(mine):
        return lax.all_to_all(mine.astype(BF).reshape(ny * nz, rb, width), ("y", "z"), 0, 0)

    def gather_yz(spread):
        return lax.all_to_all(spread, ("y", "z"), 0, 0).reshape(ny, half, width)

    gathered0 = lax.all_gather(panels[0], "x", axis=0, tiled=True)

    table = jnp.concatenate([left.reshape(4, rows), right.reshape(4, rows), pivots[None]], axis=0)
    table = jnp.pad(table, ((0, 7), (0, 0))).T

    few = table[:low].reshape(2, rb, 16).transpose(1, 2, 0).reshape(rb, 32)
    few = jnp.concatenate(two_parts(few), axis=1)
    few = jnp.pad(few, ((0, 0), (0, half - few.shape[1])))
    blocks = inverse.reshape(2, rb, ny, 2, half)
    wide0 = blocks[0].transpose(1, 2, 0, 3)[:, :, None]
    wide1 = jnp.broadcast_to(blocks[1].transpose(1, 2, 0, 3)[:, None], (ny, 2, 2, rb, half))
    shared = jnp.concatenate([rhs[:low].reshape(2, rb, half), few[None]], axis=0)
    shared = jnp.broadcast_to(shared[None, None], (ny, 2, 3, rb, half))
    message = jnp.concatenate([wide0, wide1, shared], axis=2).reshape(ny * 2, 6, rb, half)
    arrived = lax.all_to_all(message, ("y", "c"), 0, 0)

    to_owner = [(i, (i % nz) * 2 + i // nz) for i in range(2 * nz)]
    own_pivots = lax.ppermute(
        jnp.broadcast_to(table[:low, PIV:PIV + 1], (low, width)), ("z", "c"), to_owner)

    shape = jax.ShapeDtypeStruct
    whole, sent = shape((rows, width), F32), shape((rows, width), BF)
    send = elementwise(left_send, sent, rhs, table)
    got = swap_y(send, outer, ny)
    arrived, got, own_pivots = lax.optimization_barrier((arrived, got, own_pivots))
    value, send = elementwise(left_middle, (whole, sent), rhs, got, table)
    crossed = swap_y(send, inner, ny)

    small = arrived[:, 5].astype(F32)
    small = small[:, :, :32] + small[:, :, 32:64]
    tile0 = arrived[:, 0].reshape(chunk, half)
    tile1 = jnp.concatenate(
        [arrived[:, 1].reshape(chunk, half), arrived[:, 2].reshape(chunk, half)], axis=1)

    part, x1 = pl.pallas_call(
        lambda *refs: start_bands(ny, outer, inner, *refs),
        out_shape=(shape((half, width), BF), shape((ny * 2, rb, width), F32)),
    )(small, arrived)
    x1 = lax.dynamic_slice_in_dim(x1, 2 * y, 2, 0).reshape(low, width)

    own0, spread = spread_sum(lax.all_to_all(part.reshape(nz, rb, width), "z", 0, 0), ny * nz)
    spread, second = lax.optimization_barrier((spread, panels[1]))
    gathered1 = lax.all_gather(second, "x", axis=0, tiled=True)
    mine0 = gather_yz(spread)
    mine0, crossed = lax.optimization_barrier((mine0, crossed))

    core_spec = pl.BlockSpec(memory_space=pltpu.SMEM)
    vmem = pl.BlockSpec(memory_space=pltpu.VMEM)
    cross = gathered0[rb:low]
    spread = pl.pallas_call(
        second_input, out_shape=shape((ny, low, width), BF),
        in_specs=[core_spec] + [vmem] * 4, out_specs=vmem,
        scratch_shapes=[pltpu.VMEM((low, band), BF)],
    )(core_ref, x1, cross, swap_core(cross), mine0)
    x1 = lax.all_to_all(spread, "y", 0, 0).reshape(chunk, width)
    other0 = swap_core(mine0)
    part = down(tile1, x1).astype(BF).reshape(2 * nz, rb, width)
    met = lax.all_to_all(part, ("c", "z"), 0, 0)
    met, other0 = lax.optimization_barrier((met, other0))
    own1, spread = spread_sum(met, ny * nz)

    tile = rows // 3
    steps = rows // tile
    panel_spec = pl.BlockSpec((tile, band), lambda i: (i, 0))
    row_spec = pl.BlockSpec((tile, width), lambda i: (i, 0))
    table_spec = pl.BlockSpec((tile, 16), lambda i: (i, 0))
    half_spec = pl.BlockSpec((ny, half, width), lambda i: (0, 0, 0))
    params = pltpu.CompilerParams(vmem_limit_bytes=40 * 2 ** 20)
    cost = pl.CostEstimate(
        flops=2 * rows * band * width, bytes_accessed=2 * rows * band, transcendentals=0)
    solved_ref = pltpu.VMEM((band, width), BF)
    base = pl.pallas_call(
        first_update, out_shape=whole, grid=(steps,),
        in_specs=[core_spec, panel_spec, half_spec, half_spec, row_spec, row_spec],
        out_specs=row_spec, scratch_shapes=[solved_ref],
        compiler_params=params, cost_estimate=cost,
    )(core_ref, gathered0, mine0, other0, value, crossed)

    mine1 = gather_yz(spread)
    mine1, base, cross = lax.optimization_barrier((mine1, base, cross))
    cross = lax.all_gather(cross, ("y", "c"), axis=0, tiled=True)
    other1 = swap_core(mine1)
    halves = (shape((ny, half, width), F32), shape((ny, half, width), BF))
    scaled, rounded, term1, away1 = pl.pallas_call(
        lambda *refs: middle(low, tile, *refs),
        out_shape=(whole, sent) + halves, grid=(steps,),
        in_specs=[core_spec, panel_spec, half_spec, half_spec, row_spec, table_spec],
        out_specs=(row_spec, row_spec, half_spec, half_spec),
        scratch_shapes=[pltpu.VMEM((width, band), F32), solved_ref],
        compiler_params=params, cost_estimate=cost,
    )(core_ref, gathered1, mine1, other1, base, table)
    met = reduce_yz(term1 + swap_core(away1).astype(F32))

    got = swap_y(rounded, inner, ny)
    term0, away0 = pl.pallas_call(
        first_term, out_shape=halves, grid=(steps,),
        in_specs=[core_spec, panel_spec, row_spec], out_specs=(half_spec, half_spec),
        scratch_shapes=[pltpu.VMEM((width, band), F32)],
        compiler_params=params, cost_estimate=cost,
    )(core_ref, gathered0, rounded)
    away0 = swap_core(away0)
    met, got, term0, away0, cross = lax.optimization_barrier((met, got, term0, away0, cross))
    _, spread = spread_sum(met, 2 * nz, own1, own_pivots[rb:])

    value, send = elementwise(right_middle, (whole, sent), scaled, got, table)
    got = swap_y(send, outer, ny)
    t1 = lax.all_to_all(spread, ("c", "z"), 0, 0).reshape(2 * half, width)
    back1, term0 = pl.pallas_call(
        cross_back, out_shape=(shape((chunk, width), F32), shape((ny, half, width), BF)),
        in_specs=[core_spec] + [vmem] * 5, out_specs=(vmem, vmem),
        compiler_params=params,
    )(core_ref, tile1, t1, cross, term0, away0)
    met = reduce_yz(term0)
    met, got = lax.optimization_barrier((met, got))
    _, spread = spread_sum(met, nz, own0, own_pivots[:rb])
    out = elementwise(right_end, whole, value, got, table)
    t0 = lax.all_to_all(spread, "z", 0, 0).reshape(half, width)
    t0, out = lax.optimization_barrier((t0, out))
    last = pl.pallas_call(
        lambda *refs: end_bands(ny, outer, inner, *refs),
        out_shape=shape((ny * 2, low, width), BF),
        in_specs=[core_spec] + [vmem] * 4, out_specs=vmem,
    )(core_ref, small, tile0, t0, back1)
    head = total(lax.all_to_all(last, ("y", "c"), 0, 0))
    return lax.dynamic_update_slice(out, head, (0, 0))


def solution(mesh):
    rows, cols = mesh.devices.shape
    grid = Mesh(mesh.devices.reshape(grid_of(rows) + (cols,)), ("y", "z", "c", "x"))
    in_specs = (
        P(ROWS, "x"),
        P(None, None, ROWS),
        P(None, None, ROWS),
        P(ROWS),
        P(None, ROWS + ("x",), None),
        P(None, ROWS, None),
    )
    return jax.shard_map(
        shards, mesh=grid, in_specs=in_specs, out_specs=P(ROWS, "x"), check_vma=False)
```

```python
import jax
import jax.numpy as jnp
from jax import lax
from jax.experimental import pallas as pl
from jax.experimental.pallas import tpu as pltpu
from jax.sharding import Mesh, PartitionSpec as P

BF = jnp.bfloat16
F32 = jnp.float32
ROWS = ("y", "z", "c")
DOWN = (((0,), (0,)), ((), ()))


def grid_of(rows):
    z = 8 if rows >= 128 else 4
    return rows // (2 * z), z, 2


def swap_y(v, bit, count):
    return lax.ppermute(v, "y", [(i, i ^ bit) for i in range(count)])


def swap_core(v):
    return lax.ppermute(v, "c", [(0, 1), (1, 0)])


def everyone(block, axes, count):
    return lax.all_to_all(jnp.broadcast_to(block[None], (count,) + block.shape), axes, 0, 0)


def two_parts(v):
    high = v.astype(BF)
    return high, (v - high.astype(F32)).astype(BF)


def total(v):
    return jnp.sum(v.astype(F32), axis=0)


def dot(a, b):
    return jnp.dot(a, b, preferred_element_type=F32)


def down(a, b):
    return lax.dot_general(a, b, DOWN, preferred_element_type=F32)


LO, LI, RO, RI, PIV = 0, 2, 4, 6, 8


def column(table, k):
    return table[:, k:k + 1]


def elementwise(body, outs, *args):
    size = sum(a.size * a.dtype.itemsize for a in args)
    return pl.pallas_call(
        body,
        out_shape=outs,
        cost_estimate=pl.CostEstimate(flops=0, bytes_accessed=2 * size, transcendentals=0),
    )(*args)


def left_send(rhs, table, send):
    send[...] = (column(table, LO + 1) * rhs[...].astype(F32)).astype(BF)


def left_middle(rhs, got, table, value, send):
    v = column(table, LO) * rhs[...].astype(F32) + got[...].astype(F32)
    value[...] = column(table, LI) * v
    send[...] = (column(table, LI + 1) * v).astype(BF)


def right_middle(scaled, got, table, value, send):
    v = column(table, RI) * scaled[...] + column(table, RI + 1) * got[...].astype(F32)
    value[...] = column(table, RO) * v
    send[...] = v.astype(BF)


def right_end(value, got, table, out):
    out[...] = value[...] + column(table, RO + 1) * got[...].astype(F32)


def assemble(core, mine, other, solved):
    ny, half, _ = mine.shape
    for y in range(ny):
        for h in range(2):
            start = (2 * y + h) * half

            @pl.when(core[0] == h)
            def _():
                solved[start:start + half] = mine[y]

            @pl.when(core[0] != h)
            def _():
                solved[start:start + half] = other[y]


def pieces(band, quarters, rows, panel, left, right, opposite):
    held = (panel[band], left[band], right[band], opposite[...])
    return [(pl.ds(pl.multiple_of(quarters[i] * rows, rows), rows), v)
            for i, v in enumerate(held)]


def first_update(
        core, quarters, panel, left, right, opposite, mine, other, value, got, base, solved):
    assemble(core, mine, other, solved)
    rows = opposite.shape[0]
    for at, held in pieces(0, quarters, rows, panel, left, right, opposite):
        base[at] = value[at] + got[at].astype(F32) - dot(held, solved[...])


def split_term(core, acc, mine, away):
    ny, half, width = mine.shape
    for y in range(ny):
        for h in range(2):
            start = (2 * y + h) * half
            block = acc[:, start:start + half].T

            @pl.when(core[0] == h)
            def _():
                mine[y] = block

            @pl.when(core[0] != h)
            def _():
                away[y] = block.astype(BF)


def middle(
        low, core, quarters, panel, left, right, opposite, own, other, base, table,
        scaled, rounded, mine, away, acc, solved):
    assemble(core, own, other, solved)
    rows = opposite.shape[0]
    parts = pieces(1, quarters, rows, panel, left, right, opposite)
    for i, (at, held) in enumerate(parts):
        v = (base[at] - dot(held, solved[...])) / table[at, PIV:PIV + 1]
        scaled[at] = v
        row = lax.broadcasted_iota(jnp.int32, v.shape, 0) + quarters[i] * rows
        kept = jnp.where(row >= low, v, 0.0)
        rounded[at] = kept.astype(BF)
        add = dot(kept.T.astype(BF), held)
        acc[...] = add if i == 0 else acc[...] + add
    split_term(core, acc, mine, away)


def first_term(core, quarters, panel, left, right, opposite, rounded, mine, away, acc):
    rows = opposite.shape[0]
    parts = pieces(0, quarters, rows, panel, left, right, opposite)
    for i, (at, held) in enumerate(parts):
        add = dot(rounded[at].astype(F32).T.astype(BF), held)
        acc[...] = add if i == 0 else acc[...] + add
    split_term(core, acc, mine, away)


def second_input(core, x1, mine_rows, other_rows, solved, spread, cross, rows):
    ny, half, width = solved.shape
    rb = mine_rows.shape[0]
    first = jnp.where(core[0] == 0, 1.0, 0.0)

    @pl.when(core[0] == 0)
    def _():
        rows[:rb] = mine_rows[...]
        rows[rb:] = other_rows[...]

    @pl.when(core[0] != 0)
    def _():
        rows[:rb] = other_rows[...]
        rows[rb:] = mine_rows[...]

    v = first * x1[...]
    for y in range(ny):
        start = pl.multiple_of((2 * y + core[0]) * half, half)
        share = rows[:, pl.ds(start, half)]
        cross[:, y * half:(y + 1) * half] = share
        v = v - dot(share, solved[y])
    v = v.astype(BF)
    for y in range(ny):
        spread[y] = v


def cross_back(core, tile, target, cross, term, away, back, out, turned):
    ny, half, _ = term.shape
    back[...] = dot(tile[...], target[...])
    low = back.shape[0] // ny
    for k in range(ny):
        at = pl.ds(pl.multiple_of((core[1] ^ k) * low, low), low)
        turned[k * low:(k + 1) * low] = back[at]
    v = turned[...].T.astype(BF)
    for y in range(ny):
        share = dot(v, cross[:, y * half:(y + 1) * half]).T
        out[y] = (term[y] + away[y].astype(F32) + share).astype(BF)


def end_bands(ny, outer, inner, core, coefs, tile, target, back1, last):
    n, rb = coefs.shape[:2]
    first = jnp.where(core[0] == 0, 1.0, 0.0)
    values = [dot(tile[...], target[...]), first * back1[...]]
    for b in range(2):
        v = [values[b][i * rb:(i + 1) * rb] for i in range(n)]
        for level, bit in ((RI, 2 * inner), (RO, 2 * outer)):
            k = 2 * level + b
            v = [coefs[i][:, k:k + 1] * v[i] + coefs[i][:, k + 2:k + 3] * v[i ^ bit]
                 for i in range(n)]
        for i in range(n):
            last[i, b * rb:(b + 1) * rb] = v[i].astype(BF)


def spread_sum(arrived, count, base=None, pivots=None):
    rb, width = arrived.shape[1:]

    def body(*refs):
        own, spread = refs[-2:]
        v = jnp.sum(refs[0][...].astype(F32), axis=0)
        if base is not None:
            v = refs[1][...] / refs[2][...] - v
        own[...] = v
        v = v.astype(BF)
        for i in range(count):
            spread[i] = v

    args = (arrived,) if base is None else (arrived, base, pivots)
    return pl.pallas_call(
        body,
        out_shape=(jax.ShapeDtypeStruct((rb, width), F32),
                   jax.ShapeDtypeStruct((count, rb, width), BF)),
        cost_estimate=pl.CostEstimate(
            flops=0, bytes_accessed=2 * arrived.size, transcendentals=0),
    )(*args)


def start_bands(ny, outer, inner, coefs, arrived, part, x1):
    rb, width = arrived.shape[2:]
    n = 2 * ny

    def fly(b, i, level, v):
        bit = (outer if level == 0 else inner) * 2
        own = level * 4 + b
        j = i ^ bit
        a = coefs[i][:, own:own + 1] * v[i]
        return a + coefs[j][:, own + 2:own + 3] * v[j]

    both = []
    for b in range(2):
        raw = [arrived[i, 3 + b].astype(F32) for i in range(n)]
        first = [fly(b, i, 0, raw) for i in range(n)]
        both.append([fly(b, i, 1, first) for i in range(n)])
    tile = jnp.concatenate([arrived[i, 0] for i in range(n)], axis=0)
    x0 = jnp.concatenate(both[0], axis=0).astype(BF)
    part[...] = down(tile, x0).astype(BF)
    for i in range(n):
        x1[i] = both[1][i]


def shards(rhs, left, right, pivots, panels, inverse):
    ny, nz = lax.axis_size("y"), lax.axis_size("z")
    rb, band = inverse.shape[1], inverse.shape[2]
    rows, width = rhs.shape
    half = nz * rb
    low = 2 * rb
    core, y = lax.axis_index("c"), lax.axis_index("y")
    outer, inner = ny // 2, ny // 4
    chunk = ny * 2 * rb
    core_ref = jnp.stack([core, y]).astype(jnp.int32)

    def reduce_yz(mine):
        return lax.all_to_all(mine.astype(BF).reshape(ny * nz, rb, width), ("y", "z"), 0, 0)

    def gather_yz(spread):
        return lax.all_to_all(spread, ("y", "z"), 0, 0).reshape(ny, half, width)

    x, nx = lax.axis_index("x"), lax.axis_size("x")
    forward = [(i, (i + 1) % nx) for i in range(nx)]
    backward = [(i, (i - 1) % nx) for i in range(nx)]
    from_left = lax.ppermute(panels, "x", forward)
    from_right = lax.ppermute(panels, "x", backward)
    quarters = jnp.stack([x, x + nx - 1, x + 1, x + 2]).astype(jnp.int32) % nx
    table = jnp.concatenate([left.reshape(4, rows), right.reshape(4, rows), pivots[None]], axis=0)
    table = jnp.pad(table, ((0, 7), (0, 0))).T

    few = table[:low].reshape(2, rb, 16).transpose(1, 2, 0).reshape(rb, 32)
    few = jnp.concatenate(two_parts(few), axis=1)
    few = jnp.pad(few, ((0, 0), (0, half - few.shape[1])))
    blocks = inverse.reshape(2, rb, ny, 2, half)
    wide0 = blocks[0].transpose(1, 2, 0, 3)[:, :, None]
    wide1 = jnp.broadcast_to(blocks[1].transpose(1, 2, 0, 3)[:, None], (ny, 2, 2, rb, half))
    shared = jnp.concatenate([rhs[:low].reshape(2, rb, half), few[None]], axis=0)
    shared = jnp.broadcast_to(shared[None, None], (ny, 2, 3, rb, half))
    message = jnp.concatenate([wide0, wide1, shared], axis=2).reshape(ny * 2, 6, rb, half)
    arrived = lax.all_to_all(message, ("y", "c"), 0, 0)

    to_owner = [(i, (i % nz) * 2 + i // nz) for i in range(2 * nz)]
    own_pivots = lax.ppermute(
        jnp.broadcast_to(table[:low, PIV:PIV + 1], (low, width)), ("z", "c"), to_owner)

    shape = jax.ShapeDtypeStruct
    whole, sent = shape((rows, width), F32), shape((rows, width), BF)
    send = elementwise(left_send, sent, rhs, table)
    arrived, send, own_pivots = lax.optimization_barrier((arrived, send, own_pivots))
    got = swap_y(send, outer, ny)

    small = arrived[:, 5].astype(F32)
    small = small[:, :, :32] + small[:, :, 32:64]
    tile0 = arrived[:, 0].reshape(chunk, half)
    tile1 = jnp.concatenate(
        [arrived[:, 1].reshape(chunk, half), arrived[:, 2].reshape(chunk, half)], axis=1)

    part, x1 = pl.pallas_call(
        lambda *refs: start_bands(ny, outer, inner, *refs),
        out_shape=(shape((half, width), BF), shape((ny * 2, rb, width), F32)),
    )(small, arrived)
    x1 = lax.dynamic_slice_in_dim(x1, 2 * y, 2, 0).reshape(low, width)

    own0, spread = spread_sum(lax.all_to_all(part.reshape(nz, rb, width), "z", 0, 0), ny * nz)
    spread, from_left, from_right = lax.optimization_barrier((spread, from_left, from_right))
    held = (panels, from_left, from_right)
    opposite0 = lax.ppermute(from_left[0], "x", forward)
    opposite1 = lax.ppermute(from_right[1], "x", backward)
    mine0 = gather_yz(spread)
    mine0, got = lax.optimization_barrier((mine0, got))
    value, send = elementwise(left_middle, (whole, sent), rhs, got, table)
    crossed = swap_y(send, inner, ny)

    core_spec = pl.BlockSpec(memory_space=pltpu.SMEM)
    vmem = pl.BlockSpec(memory_space=pltpu.VMEM)
    cross = opposite0[rb:low]
    for quarter, source in ((0, panels), (1, from_left), (nx - 1, from_right)):
        cross = jnp.where(x == quarter, source[0, rb:low], cross)
    spread, cross = pl.pallas_call(
        second_input,
        out_shape=(shape((ny, low, width), BF), shape((low, ny * half), BF)),
        in_specs=[core_spec] + [vmem] * 4, out_specs=(vmem, vmem),
        scratch_shapes=[pltpu.VMEM((low, band), BF)],
    )(core_ref, x1, cross, swap_core(cross), mine0)
    x1 = lax.all_to_all(spread, "y", 0, 0).reshape(chunk, width)
    def doubled(v, bit):
        return jnp.concatenate([v, swap_y(v, bit, ny)], axis=0)

    cross = doubled(cross, 1)
    other0 = swap_core(mine0)
    part = down(tile1, x1).astype(BF).reshape(2 * nz, rb, width)
    met = lax.all_to_all(part, ("c", "z"), 0, 0)
    met, other0, cross, crossed = lax.optimization_barrier((met, other0, cross, crossed))
    own1, spread = spread_sum(met, ny * nz)

    params = pltpu.CompilerParams(vmem_limit_bytes=40 * 2 ** 20)
    cost = pl.CostEstimate(
        flops=2 * rows * band * width, bytes_accessed=2 * rows * band, transcendentals=0)
    solved_ref = pltpu.VMEM((band, width), BF)
    base = pl.pallas_call(
        first_update, out_shape=whole,
        in_specs=[core_spec] * 2 + [vmem] * 8, out_specs=vmem, scratch_shapes=[solved_ref],
        compiler_params=params, cost_estimate=cost,
    )(core_ref, quarters, *held, opposite0, mine0, other0, value, crossed)

    mine1 = gather_yz(spread)
    cross = doubled(cross, 2)
    mine1, base, opposite1, cross = lax.optimization_barrier((mine1, base, opposite1, cross))
    other1 = swap_core(mine1)
    halves = (shape((ny, half, width), F32), shape((ny, half, width), BF))
    scaled, rounded, term1, away1 = pl.pallas_call(
        lambda *refs: middle(low, *refs),
        out_shape=(whole, sent) + halves,
        in_specs=[core_spec] * 2 + [vmem] * 8, out_specs=(vmem,) * 4,
        scratch_shapes=[pltpu.VMEM((width, band), F32), solved_ref],
        compiler_params=params, cost_estimate=cost,
    )(core_ref, quarters, *held, opposite1, mine1, other1, base, table)
    met = reduce_yz(term1 + swap_core(away1).astype(F32))

    term0, away0 = pl.pallas_call(
        first_term, out_shape=halves,
        in_specs=[core_spec] * 2 + [vmem] * 5, out_specs=(vmem,) * 2,
        scratch_shapes=[pltpu.VMEM((width, band), F32)],
        compiler_params=params, cost_estimate=cost,
    )(core_ref, quarters, *held, opposite0, rounded)
    away0 = swap_core(away0)
    if ny > 4:
        cross = doubled(cross, 4)
    met, rounded, term0, away0, cross = lax.optimization_barrier(
        (met, rounded, term0, away0, cross))
    _, spread = spread_sum(met, 2 * nz, own1, own_pivots[rb:])

    got = swap_y(rounded, inner, ny)
    t1 = lax.all_to_all(spread, ("c", "z"), 0, 0).reshape(2 * half, width)
    t1, got = lax.optimization_barrier((t1, got))
    back1, term0 = pl.pallas_call(
        cross_back, out_shape=(shape((chunk, width), F32), shape((ny, half, width), BF)),
        in_specs=[core_spec] + [vmem] * 5, out_specs=(vmem, vmem),
        scratch_shapes=[pltpu.VMEM((chunk, width), F32)], compiler_params=params,
    )(core_ref, tile1, t1, cross, term0, away0)
    met = reduce_yz(term0)
    value, send = elementwise(right_middle, (whole, sent), scaled, got, table)
    met, send = lax.optimization_barrier((met, send))
    _, spread = spread_sum(met, nz, own0, own_pivots[:rb])
    t0 = lax.all_to_all(spread, "z", 0, 0).reshape(half, width)
    t0, got = lax.optimization_barrier((t0, swap_y(send, outer, ny)))
    out = elementwise(right_end, whole, value, got, table)
    last = pl.pallas_call(
        lambda *refs: end_bands(ny, outer, inner, *refs),
        out_shape=shape((ny * 2, low, width), BF),
        in_specs=[core_spec] + [vmem] * 4, out_specs=vmem,
    )(core_ref, small, tile0, t0, back1)
    met, out = lax.optimization_barrier((lax.all_to_all(last, ("y", "c"), 0, 0), out))
    head = total(met)
    return lax.dynamic_update_slice(out, head, (0, 0))


def solution(mesh):
    rows, cols = mesh.devices.shape
    grid = Mesh(mesh.devices.reshape(grid_of(rows) + (cols,)), ("y", "z", "c", "x"))
    in_specs = (
        P(ROWS, "x"),
        P(None, None, ROWS),
        P(None, None, ROWS),
        P(ROWS),
        P(None, ROWS + ("x",), None),
        P(None, ROWS, None),
    )
    return jax.shard_map(
        shards, mesh=grid, in_specs=in_specs, out_specs=P(ROWS, "x"), check_vma=False)
```

```python
import jax
import jax.numpy as jnp
from jax import lax
from jax.experimental import pallas as pl
from jax.experimental.pallas import tpu as pltpu
from jax.sharding import Mesh, PartitionSpec as P

BF = jnp.bfloat16
F32 = jnp.float32
ROWS = ("y", "z", "c")
DOWN = (((0,), (0,)), ((), ()))


def limit(mib):
    return pltpu.CompilerParams(vmem_limit_bytes=mib * 2 ** 20)


def grid_of(rows):
    z = 8 if rows >= 128 else 4
    return rows // (2 * z), z, 2


def swap_y(v, bit, count):
    return lax.ppermute(v, "y", [(i, i ^ bit) for i in range(count)])


def swap_core(v):
    return lax.ppermute(v, "c", [(0, 1), (1, 0)])


def everyone(block, axes, count):
    return lax.all_to_all(jnp.broadcast_to(block[None], (count,) + block.shape), axes, 0, 0)


def two_parts(v):
    high = v.astype(BF)
    return high, (v - high.astype(F32)).astype(BF)


def total(v):
    return jnp.sum(v.astype(F32), axis=0)


def dot(a, b):
    return jnp.dot(a, b, preferred_element_type=F32)


def down(a, b):
    return lax.dot_general(a, b, DOWN, preferred_element_type=F32)


LO, LI, RO, RI, PIV = 0, 2, 4, 6, 8


def column(table, k):
    return table[:, k:k + 1]


def elementwise(body, outs, *args):
    size = sum(a.size * a.dtype.itemsize for a in args)
    return pl.pallas_call(
        body,
        out_shape=outs,
        compiler_params=limit(6),
        cost_estimate=pl.CostEstimate(flops=0, bytes_accessed=2 * size, transcendentals=0),
    )(*args)


def left_send(rhs, table, send):
    send[...] = (column(table, LO + 1) * rhs[...].astype(F32)).astype(BF)


def left_middle(rhs, got, table, value, send):
    v = column(table, LO) * rhs[...].astype(F32) + got[...].astype(F32)
    value[...] = column(table, LI) * v
    send[...] = (column(table, LI + 1) * v).astype(BF)


def right_middle(scaled, got, table, value, send):
    v = column(table, RI) * scaled[...] + column(table, RI + 1) * got[...].astype(F32)
    value[...] = column(table, RO) * v
    send[...] = v.astype(BF)


def right_end(value, got, table, out):
    out[...] = value[...] + column(table, RO + 1) * got[...].astype(F32)


def assemble(core, mine, other, solved):
    ny, half, _ = mine.shape
    for y in range(ny):
        for h in range(2):
            start = (2 * y + h) * half

            @pl.when(core[0] == h)
            def _():
                solved[start:start + half] = mine[y]

            @pl.when(core[0] != h)
            def _():
                solved[start:start + half] = other[y]


def first_update(core, panel, mine, other, value, got, base, solved):
    @pl.when(pl.program_id(0) == 0)
    def _():
        assemble(core, mine, other, solved)

    base[...] = value[...] + got[...].astype(F32) - dot(panel[...], solved[...])


def split_term(core, acc, mine, away):
    ny, half, width = mine.shape
    for y in range(ny):
        for h in range(2):
            start = (2 * y + h) * half
            block = acc[:, start:start + half].T

            @pl.when(core[0] == h)
            def _():
                mine[y] = block

            @pl.when(core[0] != h)
            def _():
                away[y] = block.astype(BF)


def middle(
        low, tile, core, panel, own, other, base, table, scaled, rounded, mine, away, acc, solved):
    step = pl.program_id(0)

    @pl.when(step == 0)
    def _():
        assemble(core, own, other, solved)

    v = (base[...] - dot(panel[...], solved[...])) / column(table, PIV)
    scaled[...] = v
    row = lax.broadcasted_iota(jnp.int32, v.shape, 0) + step * tile
    kept = jnp.where(row >= low, v, 0.0)
    rounded[...] = kept.astype(BF)
    add = dot(kept.T.astype(BF), panel[...])

    @pl.when(step == 0)
    def _():
        acc[...] = add

    @pl.when(step > 0)
    def _():
        acc[...] += add

    @pl.when(step == pl.num_programs(0) - 1)
    def _():
        split_term(core, acc, mine, away)


def first_term(core, panel, rounded, mine, away, acc):
    step = pl.program_id(0)
    add = dot(rounded[...].astype(F32).T.astype(BF), panel[...])

    @pl.when(step == 0)
    def _():
        acc[...] = add

    @pl.when(step > 0)
    def _():
        acc[...] += add

    @pl.when(step == pl.num_programs(0) - 1)
    def _():
        split_term(core, acc, mine, away)


def second_input(core, x1, mine_rows, other_rows, solved, spread, rows):
    ny, half, width = solved.shape
    rb = mine_rows.shape[0]
    first = jnp.where(core[0] == 0, 1.0, 0.0)

    @pl.when(core[0] == 0)
    def _():
        rows[:rb] = mine_rows[...]
        rows[rb:] = other_rows[...]

    @pl.when(core[0] != 0)
    def _():
        rows[:rb] = other_rows[...]
        rows[rb:] = mine_rows[...]

    v = first * x1[...]
    for y in range(ny):
        start = pl.multiple_of((2 * y + core[0]) * half, half)
        v = v - dot(rows[:, pl.ds(start, half)], solved[y])
    v = v.astype(BF)
    for y in range(ny):
        spread[y] = v


def cross_back(core, tile, target, cross, term, away, back, out):
    ny, half, _ = term.shape
    v = dot(tile[...], target[...])
    back[...] = v
    turned = v.T.astype(BF)
    for y in range(ny):
        start = pl.multiple_of((2 * y + core[0]) * half, half)
        share = dot(turned, cross[:, pl.ds(start, half)]).T
        out[y] = (term[y] + away[y].astype(F32) + share).astype(BF)


def end_bands(ny, outer, inner, core, coefs, tile, target, back1, last):
    n, rb = coefs.shape[:2]
    first = jnp.where(core[0] == 0, 1.0, 0.0)
    values = [dot(tile[...], target[...]), first * back1[...]]
    for b in range(2):
        v = [values[b][i * rb:(i + 1) * rb] for i in range(n)]
        for level, bit in ((RI, 2 * inner), (RO, 2 * outer)):
            k = 2 * level + b
            v = [coefs[i][:, k:k + 1] * v[i] + coefs[i][:, k + 2:k + 3] * v[i ^ bit]
                 for i in range(n)]
        for i in range(n):
            last[i, b * rb:(b + 1) * rb] = v[i].astype(BF)


def spread_sum(arrived, count, base=None, pivots=None):
    rb, width = arrived.shape[1:]

    def body(*refs):
        own, spread = refs[-2:]
        v = jnp.sum(refs[0][...].astype(F32), axis=0)
        if base is not None:
            v = refs[1][...] / refs[2][...] - v
        own[...] = v
        v = v.astype(BF)
        for i in range(count):
            spread[i] = v

    args = (arrived,) if base is None else (arrived, base, pivots)
    return pl.pallas_call(
        body,
        out_shape=(jax.ShapeDtypeStruct((rb, width), F32),
                   jax.ShapeDtypeStruct((count, rb, width), BF)),
        cost_estimate=pl.CostEstimate(
            flops=0, bytes_accessed=2 * arrived.size, transcendentals=0),
        compiler_params=limit(4),
    )(*args)


def start_bands(ny, outer, inner, coefs, arrived, part, x1):
    rb, width = arrived.shape[2:]
    n = 2 * ny

    def fly(b, i, level, v):
        bit = (outer if level == 0 else inner) * 2
        own = level * 4 + b
        j = i ^ bit
        a = coefs[i][:, own:own + 1] * v[i]
        return a + coefs[j][:, own + 2:own + 3] * v[j]

    both = []
    for b in range(2):
        raw = [arrived[i, 3 + b].astype(F32) for i in range(n)]
        first = [fly(b, i, 0, raw) for i in range(n)]
        both.append([fly(b, i, 1, first) for i in range(n)])
    tile = jnp.concatenate([arrived[i, 0] for i in range(n)], axis=0)
    x0 = jnp.concatenate(both[0], axis=0).astype(BF)
    part[...] = down(tile, x0).astype(BF)
    for i in range(n):
        x1[i] = both[1][i]


def shards(rhs, left, right, pivots, panels, inverse):
    ny, nz = lax.axis_size("y"), lax.axis_size("z")
    rb, band = inverse.shape[1], inverse.shape[2]
    rows, width = rhs.shape
    half = nz * rb
    low = 2 * rb
    core, y = lax.axis_index("c"), lax.axis_index("y")
    outer, inner = ny // 2, ny // 4
    chunk = ny * 2 * rb
    core_ref = core.astype(jnp.int32)[None]

    def reduce_yz(mine):
        return lax.all_to_all(mine.astype(BF).reshape(ny * nz, rb, width), ("y", "z"), 0, 0)

    def gather_yz(spread):
        return lax.all_to_all(spread, ("y", "z"), 0, 0).reshape(ny, half, width)

    gathered0 = lax.all_gather(panels[0], "x", axis=0, tiled=True)

    table = jnp.concatenate([left.reshape(4, rows), right.reshape(4, rows), pivots[None]], axis=0)
    table = jnp.pad(table, ((0, 7), (0, 0))).T

    few = table[:low].reshape(2, rb, 16).transpose(1, 2, 0).reshape(rb, 32)
    few = jnp.concatenate(two_parts(few), axis=1)
    few = jnp.pad(few, ((0, 0), (0, half - few.shape[1])))
    blocks = inverse.reshape(2, rb, ny, 2, half)
    wide0 = blocks[0].transpose(1, 2, 0, 3)[:, :, None]
    wide1 = jnp.broadcast_to(blocks[1].transpose(1, 2, 0, 3)[:, None], (ny, 2, 2, rb, half))
    shared = jnp.concatenate([rhs[:low].reshape(2, rb, half), few[None]], axis=0)
    shared = jnp.broadcast_to(shared[None, None], (ny, 2, 3, rb, half))
    message = jnp.concatenate([wide0, wide1, shared], axis=2).reshape(ny * 2, 6, rb, half)
    arrived = lax.all_to_all(message, ("y", "c"), 0, 0)

    to_owner = [(i, (i % nz) * 2 + i // nz) for i in range(2 * nz)]
    own_pivots = lax.ppermute(
        jnp.broadcast_to(table[:low, PIV:PIV + 1], (low, width)), ("z", "c"), to_owner)

    shape = jax.ShapeDtypeStruct
    whole, sent = shape((rows, width), F32), shape((rows, width), BF)
    send = elementwise(left_send, sent, rhs, table)
    arrived, own_pivots, send = lax.optimization_barrier((arrived, own_pivots, send))
    got = swap_y(send, outer, ny)

    small = arrived[:, 5].astype(F32)
    small = small[:, :, :32] + small[:, :, 32:64]
    tile0 = arrived[:, 0].reshape(chunk, half)
    tile1 = jnp.concatenate(
        [arrived[:, 1].reshape(chunk, half), arrived[:, 2].reshape(chunk, half)], axis=1)

    part, x1 = pl.pallas_call(
        lambda *refs: start_bands(ny, outer, inner, *refs),
        out_shape=(shape((half, width), BF), shape((ny * 2, rb, width), F32)),
        compiler_params=limit(8),
    )(small, arrived)
    x1 = lax.dynamic_slice_in_dim(x1, 2 * y, 2, 0).reshape(low, width)

    met = lax.all_to_all(part.reshape(nz, rb, width), "z", 0, 0)
    met, got = lax.optimization_barrier((met, got))
    own0, spread = spread_sum(met, ny * nz)
    spread, second = lax.optimization_barrier((spread, panels[1]))
    gathered1 = lax.all_gather(second, "x", axis=0, tiled=True)
    mine0 = gather_yz(spread)
    mine0, got = lax.optimization_barrier((mine0, got))
    value, send = elementwise(left_middle, (whole, sent), rhs, got, table)
    crossed = swap_y(send, inner, ny)

    core_spec = pl.BlockSpec(memory_space=pltpu.SMEM)
    vmem = pl.BlockSpec(memory_space=pltpu.VMEM)
    cross = gathered0[rb:low]
    spread = pl.pallas_call(
        second_input, out_shape=shape((ny, low, width), BF),
        in_specs=[core_spec] + [vmem] * 4, out_specs=vmem,
        scratch_shapes=[pltpu.VMEM((low, band), BF)], compiler_params=limit(6),
    )(core_ref, x1, cross, swap_core(cross), mine0)
    x1 = lax.all_to_all(spread, "y", 0, 0).reshape(chunk, width)
    other0 = swap_core(mine0)
    part = down(tile1, x1).astype(BF).reshape(2 * nz, rb, width)
    met = lax.all_to_all(part, ("c", "z"), 0, 0)
    met, other0 = lax.optimization_barrier((met, other0))
    own1, spread = spread_sum(met, ny * nz)

    tile = rows // 3
    steps = rows // tile
    panel_spec = pl.BlockSpec((tile, band), lambda i: (i, 0))
    row_spec = pl.BlockSpec((tile, width), lambda i: (i, 0))
    table_spec = pl.BlockSpec((tile, 16), lambda i: (i, 0))
    half_spec = pl.BlockSpec((ny, half, width), lambda i: (0, 0, 0))
    params = limit(20)
    cost = pl.CostEstimate(
        flops=2 * rows * band * width, bytes_accessed=2 * rows * band, transcendentals=0)
    solved_ref = pltpu.VMEM((band, width), BF)
    base = pl.pallas_call(
        first_update, out_shape=whole, grid=(steps,),
        in_specs=[core_spec, panel_spec, half_spec, half_spec, row_spec, row_spec],
        out_specs=row_spec, scratch_shapes=[solved_ref],
        compiler_params=params, cost_estimate=cost,
    )(core_ref, gathered0, mine0, other0, value, crossed)

    mine1 = gather_yz(spread)
    mine1, base, cross, gathered1 = lax.optimization_barrier((mine1, base, cross, gathered1))
    cross = lax.all_gather(cross, ("y", "c"), axis=0, tiled=True)
    other1 = swap_core(mine1)
    halves = (shape((ny, half, width), F32), shape((ny, half, width), BF))
    scaled, rounded, term1, away1 = pl.pallas_call(
        lambda *refs: middle(low, tile, *refs),
        out_shape=(whole, sent) + halves, grid=(steps,),
        in_specs=[core_spec, panel_spec, half_spec, half_spec, row_spec, table_spec],
        out_specs=(row_spec, row_spec, half_spec, half_spec),
        scratch_shapes=[pltpu.VMEM((width, band), F32), solved_ref],
        compiler_params=params, cost_estimate=cost,
    )(core_ref, gathered1, mine1, other1, base, table)
    met = reduce_yz(term1 + swap_core(away1).astype(F32))

    term0, away0 = pl.pallas_call(
        first_term, out_shape=halves, grid=(steps,),
        in_specs=[core_spec, panel_spec, row_spec], out_specs=(half_spec, half_spec),
        scratch_shapes=[pltpu.VMEM((width, band), F32)],
        compiler_params=params, cost_estimate=cost,
    )(core_ref, gathered0, rounded)
    away0 = swap_core(away0)
    met, rounded, term0, away0 = lax.optimization_barrier((met, rounded, term0, away0))
    _, spread = spread_sum(met, 2 * nz, own1, own_pivots[rb:])

    got = swap_y(rounded, inner, ny)
    t1 = lax.all_to_all(spread, ("c", "z"), 0, 0).reshape(2 * half, width)
    t1, got, cross = lax.optimization_barrier((t1, got, cross))
    value, send = elementwise(right_middle, (whole, sent), scaled, got, table)
    back1, term0 = pl.pallas_call(
        cross_back, out_shape=(shape((chunk, width), F32), shape((ny, half, width), BF)),
        in_specs=[core_spec] + [vmem] * 5, out_specs=(vmem, vmem),
        compiler_params=params,
    )(core_ref, tile1, t1, cross, term0, away0)
    met = reduce_yz(term0)
    met, send = lax.optimization_barrier((met, send))
    _, spread = spread_sum(met, nz, own0, own_pivots[:rb])
    t0 = lax.all_to_all(spread, "z", 0, 0).reshape(half, width)
    t0, got = lax.optimization_barrier((t0, swap_y(send, outer, ny)))
    out = elementwise(right_end, whole, value, got, table)
    last = pl.pallas_call(
        lambda *refs: end_bands(ny, outer, inner, *refs),
        out_shape=shape((ny * 2, low, width), BF),
        in_specs=[core_spec] + [vmem] * 4, out_specs=vmem, compiler_params=limit(8),
    )(core_ref, small, tile0, t0, back1)
    met, out = lax.optimization_barrier((lax.all_to_all(last, ("y", "c"), 0, 0), out))
    head = total(met)
    return lax.dynamic_update_slice(out, head, (0, 0))


def solution(mesh):
    rows, cols = mesh.devices.shape
    grid = Mesh(mesh.devices.reshape(grid_of(rows) + (cols,)), ("y", "z", "c", "x"))
    in_specs = (
        P(ROWS, "x"),
        P(None, None, ROWS),
        P(None, None, ROWS),
        P(ROWS),
        P(None, ROWS + ("x",), None),
        P(None, ROWS, None),
    )
    return jax.shard_map(
        shards, mesh=grid, in_specs=in_specs, out_specs=P(ROWS, "x"), check_vma=False)
```

```python
import jax
import jax.numpy as jnp
from jax import lax
from jax.experimental import pallas as pl
from jax.experimental.pallas import tpu as pltpu
from jax.sharding import Mesh, PartitionSpec as P

BF = jnp.bfloat16
F32 = jnp.float32
ROWS = ("y", "z", "c")
DOWN = (((0,), (0,)), ((), ()))


def limit(mib):
    return pltpu.CompilerParams(vmem_limit_bytes=mib * 2 ** 20)


def grid_of(rows):
    z = 8 if rows >= 128 else 4
    return rows // (2 * z), z, 2


def swap_y(v, bit, count):
    return lax.ppermute(v, "y", [(i, i ^ bit) for i in range(count)])


def swap_core(v):
    return lax.ppermute(v, "c", [(0, 1), (1, 0)])


def everyone(block, axes, count):
    return lax.all_to_all(jnp.broadcast_to(block[None], (count,) + block.shape), axes, 0, 0)


def two_parts(v):
    high = v.astype(BF)
    return high, (v - high.astype(F32)).astype(BF)


def total(v):
    return jnp.sum(v.astype(F32), axis=0)


def dot(a, b):
    return jnp.dot(a, b, preferred_element_type=F32)


def down(a, b):
    return lax.dot_general(a, b, DOWN, preferred_element_type=F32)


LO, LI, RO, RI, PIV = 0, 2, 4, 6, 8


def column(table, k):
    return table[:, k:k + 1]


def elementwise(body, outs, *args):
    size = sum(a.size * a.dtype.itemsize for a in args)
    return pl.pallas_call(
        body,
        out_shape=outs,
        compiler_params=limit(6),
        cost_estimate=pl.CostEstimate(flops=0, bytes_accessed=2 * size, transcendentals=0),
    )(*args)


def left_send(rhs, table, send):
    send[...] = (column(table, LO + 1) * rhs[...].astype(F32)).astype(BF)


def left_middle(rhs, got, table, value, send):
    v = column(table, LO) * rhs[...].astype(F32) + got[...].astype(F32)
    value[...] = column(table, LI) * v
    send[...] = (column(table, LI + 1) * v).astype(BF)


def right_middle(scaled, got, table, value, send):
    v = column(table, RI) * scaled[...] + column(table, RI + 1) * got[...].astype(F32)
    value[...] = column(table, RO) * v
    send[...] = v.astype(BF)


def right_end(value, got, table, out):
    out[...] = value[...] + column(table, RO + 1) * got[...].astype(F32)


def assemble(core, mine, other, solved):
    ny, half, _ = mine.shape
    for y in range(ny):
        for h in range(2):
            start = (2 * y + h) * half

            @pl.when(core[0] == h)
            def _():
                solved[start:start + half] = mine[y]

            @pl.when(core[0] != h)
            def _():
                solved[start:start + half] = other[y]


def first_update(core, panel, mine, other, value, got, base, solved):
    @pl.when(pl.program_id(0) == 0)
    def _():
        assemble(core, mine, other, solved)

    base[...] = value[...] + got[...].astype(F32) - dot(panel[...], solved[...])


def split_term(core, acc, mine, away):
    ny, half, width = mine.shape
    for y in range(ny):
        for h in range(2):
            start = (2 * y + h) * half
            block = acc[:, start:start + half].T

            @pl.when(core[0] == h)
            def _():
                mine[y] = block

            @pl.when(core[0] != h)
            def _():
                away[y] = block.astype(BF)


def middle(
        low, tile, core, panel, own, other, base, table, scaled, rounded, mine, away, acc, solved):
    step = pl.program_id(0)

    @pl.when(step == 0)
    def _():
        assemble(core, own, other, solved)

    v = (base[...] - dot(panel[...], solved[...])) / column(table, PIV)
    scaled[...] = v
    row = lax.broadcasted_iota(jnp.int32, v.shape, 0) + step * tile
    kept = jnp.where(row >= low, v, 0.0)
    rounded[...] = kept.astype(BF)
    add = dot(kept.T.astype(BF), panel[...])

    @pl.when(step == 0)
    def _():
        acc[...] = add

    @pl.when(step > 0)
    def _():
        acc[...] += add

    @pl.when(step == pl.num_programs(0) - 1)
    def _():
        split_term(core, acc, mine, away)


def first_term(core, panel, rounded, mine, away, acc):
    step = pl.program_id(0)
    add = dot(rounded[...].astype(F32).T.astype(BF), panel[...])

    @pl.when(step == 0)
    def _():
        acc[...] = add

    @pl.when(step > 0)
    def _():
        acc[...] += add

    @pl.when(step == pl.num_programs(0) - 1)
    def _():
        split_term(core, acc, mine, away)


def second_input(core, x1, mine_rows, other_rows, solved, spread, rows):
    ny, half, width = solved.shape
    rb = mine_rows.shape[0]
    first = jnp.where(core[0] == 0, 1.0, 0.0)

    @pl.when(core[0] == 0)
    def _():
        rows[:rb] = mine_rows[...]
        rows[rb:] = other_rows[...]

    @pl.when(core[0] != 0)
    def _():
        rows[:rb] = other_rows[...]
        rows[rb:] = mine_rows[...]

    v = first * x1[...]
    for y in range(ny):
        start = pl.multiple_of((2 * y + core[0]) * half, half)
        v = v - dot(rows[:, pl.ds(start, half)], solved[y])
    v = v.astype(BF)
    for y in range(ny):
        spread[y] = v


def cross_back(core, tile, target, cross, term, away, back, out):
    ny, half, _ = term.shape
    v = dot(tile[...], target[...])
    back[...] = v
    turned = v.T.astype(BF)
    for y in range(ny):
        start = pl.multiple_of((2 * y + core[0]) * half, half)
        share = dot(turned, cross[:, pl.ds(start, half)]).T
        out[y] = (term[y] + away[y].astype(F32) + share).astype(BF)


def end_bands(ny, outer, inner, core, coefs, tile, target, back1, last):
    n, rb = coefs.shape[:2]
    first = jnp.where(core[0] == 0, 1.0, 0.0)
    values = [dot(tile[...], target[...]), first * back1[...]]
    for b in range(2):
        v = [values[b][i * rb:(i + 1) * rb] for i in range(n)]
        for level, bit in ((RI, 2 * inner), (RO, 2 * outer)):
            k = 2 * level + b
            v = [coefs[i][:, k:k + 1] * v[i] + coefs[i][:, k + 2:k + 3] * v[i ^ bit]
                 for i in range(n)]
        for i in range(n):
            last[i, b * rb:(b + 1) * rb] = v[i].astype(BF)


def spread_sum(arrived, count, base=None, pivots=None):
    rb, width = arrived.shape[1:]

    def body(*refs):
        own, spread = refs[-2:]
        v = jnp.sum(refs[0][...].astype(F32), axis=0)
        if base is not None:
            v = refs[1][...] / refs[2][...] - v
        own[...] = v
        v = v.astype(BF)
        for i in range(count):
            spread[i] = v

    args = (arrived,) if base is None else (arrived, base, pivots)
    return pl.pallas_call(
        body,
        out_shape=(jax.ShapeDtypeStruct((rb, width), F32),
                   jax.ShapeDtypeStruct((count, rb, width), BF)),
        cost_estimate=pl.CostEstimate(
            flops=0, bytes_accessed=2 * arrived.size, transcendentals=0),
        compiler_params=limit(4),
    )(*args)


def start_bands(ny, outer, inner, coefs, arrived, part, x1):
    rb, width = arrived.shape[2:]
    n = 2 * ny

    def fly(b, i, level, v):
        bit = (outer if level == 0 else inner) * 2
        own = level * 4 + b
        j = i ^ bit
        a = coefs[i][:, own:own + 1] * v[i]
        return a + coefs[j][:, own + 2:own + 3] * v[j]

    both = []
    for b in range(2):
        raw = [arrived[i, 3 + b].astype(F32) for i in range(n)]
        first = [fly(b, i, 0, raw) for i in range(n)]
        both.append([fly(b, i, 1, first) for i in range(n)])
    tile = jnp.concatenate([arrived[i, 0] for i in range(n)], axis=0)
    x0 = jnp.concatenate(both[0], axis=0).astype(BF)
    part[...] = down(tile, x0).astype(BF)
    for i in range(n):
        x1[i] = both[1][i]


def shards(rhs, left, right, pivots, panels, inverse):
    ny, nz = lax.axis_size("y"), lax.axis_size("z")
    rb, band = inverse.shape[1], inverse.shape[2]
    rows, width = rhs.shape
    half = nz * rb
    low = 2 * rb
    core, y = lax.axis_index("c"), lax.axis_index("y")
    outer, inner = ny // 2, ny // 4
    chunk = ny * 2 * rb
    core_ref = core.astype(jnp.int32)[None]

    def reduce_yz(mine):
        return lax.all_to_all(mine.astype(BF).reshape(ny * nz, rb, width), ("y", "z"), 0, 0)

    def gather_yz(spread):
        return lax.all_to_all(spread, ("y", "z"), 0, 0).reshape(ny, half, width)

    gathered0 = lax.all_gather(panels[0], "x", axis=0, tiled=True)

    table = jnp.concatenate([left.reshape(4, rows), right.reshape(4, rows), pivots[None]], axis=0)
    table = jnp.pad(table, ((0, 7), (0, 0))).T

    few = table[:low].reshape(2, rb, 16).transpose(1, 2, 0).reshape(rb, 32)
    few = jnp.concatenate(two_parts(few), axis=1)
    few = jnp.pad(few, ((0, 0), (0, half - few.shape[1])))
    blocks = inverse.reshape(2, rb, ny, 2, half)
    wide0 = blocks[0].transpose(1, 2, 0, 3)[:, :, None]
    wide1 = jnp.broadcast_to(blocks[1].transpose(1, 2, 0, 3)[:, None], (ny, 2, 2, rb, half))
    shared = jnp.concatenate([rhs[:low].reshape(2, rb, half), few[None]], axis=0)
    shared = jnp.broadcast_to(shared[None, None], (ny, 2, 3, rb, half))
    message = jnp.concatenate([wide0, wide1, shared], axis=2).reshape(ny * 2, 6, rb, half)
    arrived = lax.all_to_all(message, ("y", "c"), 0, 0)

    to_owner = [(i, (i % nz) * 2 + i // nz) for i in range(2 * nz)]
    own_pivots = lax.ppermute(
        jnp.broadcast_to(table[:low, PIV:PIV + 1], (low, width)), ("z", "c"), to_owner)

    shape = jax.ShapeDtypeStruct
    whole, sent = shape((rows, width), F32), shape((rows, width), BF)
    send = elementwise(left_send, sent, rhs, table)
    arrived, own_pivots, send = lax.optimization_barrier((arrived, own_pivots, send))
    got = swap_y(send, outer, ny)

    small = arrived[:, 5].astype(F32)
    small = small[:, :, :32] + small[:, :, 32:64]
    tile0 = arrived[:, 0].reshape(chunk, half)
    tile1 = jnp.concatenate(
        [arrived[:, 1].reshape(chunk, half), arrived[:, 2].reshape(chunk, half)], axis=1)

    part, x1 = pl.pallas_call(
        lambda *refs: start_bands(ny, outer, inner, *refs),
        out_shape=(shape((half, width), BF), shape((ny * 2, rb, width), F32)),
        compiler_params=limit(8),
    )(small, arrived)
    x1 = lax.dynamic_slice_in_dim(x1, 2 * y, 2, 0).reshape(low, width)

    met = lax.all_to_all(part.reshape(nz, rb, width), "z", 0, 0)
    met, got = lax.optimization_barrier((met, got))
    own0, spread = spread_sum(met, ny * nz)
    spread, second = lax.optimization_barrier((spread, panels[1]))
    gathered1 = lax.all_gather(second, "x", axis=0, tiled=True)
    mine0 = gather_yz(spread)
    mine0, got = lax.optimization_barrier((mine0, got))
    value, send = elementwise(left_middle, (whole, sent), rhs, got, table)
    crossed = swap_y(send, inner, ny)

    core_spec = pl.BlockSpec(memory_space=pltpu.SMEM)
    vmem = pl.BlockSpec(memory_space=pltpu.VMEM)
    cross = gathered0[rb:low]
    spread = pl.pallas_call(
        second_input, out_shape=shape((ny, low, width), BF),
        in_specs=[core_spec] + [vmem] * 4, out_specs=vmem,
        scratch_shapes=[pltpu.VMEM((low, band), BF)], compiler_params=limit(6),
    )(core_ref, x1, cross, swap_core(cross), mine0)
    x1 = lax.all_to_all(spread, "y", 0, 0).reshape(chunk, width)
    other0 = swap_core(mine0)
    part = down(tile1, x1).astype(BF).reshape(2 * nz, rb, width)
    met = lax.all_to_all(part, ("c", "z"), 0, 0)
    met, other0, crossed = lax.optimization_barrier((met, other0, crossed))
    own1, spread = spread_sum(met, ny * nz)

    tile = rows // 3
    steps = rows // tile
    panel_spec = pl.BlockSpec((tile, band), lambda i: (i, 0))
    row_spec = pl.BlockSpec((tile, width), lambda i: (i, 0))
    table_spec = pl.BlockSpec((tile, 16), lambda i: (i, 0))
    half_spec = pl.BlockSpec((ny, half, width), lambda i: (0, 0, 0))
    params = limit(20)
    cost = pl.CostEstimate(
        flops=2 * rows * band * width, bytes_accessed=2 * rows * band, transcendentals=0)
    solved_ref = pltpu.VMEM((band, width), BF)
    base = pl.pallas_call(
        first_update, out_shape=whole, grid=(steps,),
        in_specs=[core_spec, panel_spec, half_spec, half_spec, row_spec, row_spec],
        out_specs=row_spec, scratch_shapes=[solved_ref],
        cost_estimate=cost,
    )(core_ref, gathered0, mine0, other0, value, crossed)

    mine1 = gather_yz(spread)
    mine1, base, cross, gathered1 = lax.optimization_barrier((mine1, base, cross, gathered1))
    cross = lax.all_gather(cross, ("y", "c"), axis=0, tiled=True)
    other1 = swap_core(mine1)
    halves = (shape((ny, half, width), F32), shape((ny, half, width), BF))
    scaled, rounded, term1, away1 = pl.pallas_call(
        lambda *refs: middle(low, tile, *refs),
        out_shape=(whole, sent) + halves, grid=(steps,),
        in_specs=[core_spec, panel_spec, half_spec, half_spec, row_spec, table_spec],
        out_specs=(row_spec, row_spec, half_spec, half_spec),
        scratch_shapes=[pltpu.VMEM((width, band), F32), solved_ref],
        cost_estimate=cost,
    )(core_ref, gathered1, mine1, other1, base, table)
    met = reduce_yz(term1 + swap_core(away1).astype(F32))

    term0, away0 = pl.pallas_call(
        first_term, out_shape=halves, grid=(steps,),
        in_specs=[core_spec, panel_spec, row_spec], out_specs=(half_spec, half_spec),
        scratch_shapes=[pltpu.VMEM((width, band), F32)],
        compiler_params=params, cost_estimate=cost,
    )(core_ref, gathered0, rounded)
    away0 = swap_core(away0)
    met, term0, away0 = lax.optimization_barrier((met, term0, away0))
    _, spread = spread_sum(met, 2 * nz, own1, own_pivots[rb:])

    got = swap_y(rounded, inner, ny)
    t1 = lax.all_to_all(spread, ("c", "z"), 0, 0).reshape(2 * half, width)
    t1, got, cross = lax.optimization_barrier((t1, got, cross))
    value, send = elementwise(right_middle, (whole, sent), scaled, got, table)
    back1, term0 = pl.pallas_call(
        cross_back, out_shape=(shape((chunk, width), F32), shape((ny, half, width), BF)),
        in_specs=[core_spec] + [vmem] * 5, out_specs=(vmem, vmem),
        compiler_params=params,
    )(core_ref, tile1, t1, cross, term0, away0)
    met = reduce_yz(term0)
    met, send = lax.optimization_barrier((met, send))
    _, spread = spread_sum(met, nz, own0, own_pivots[:rb])
    t0 = lax.all_to_all(spread, "z", 0, 0).reshape(half, width)
    t0, got = lax.optimization_barrier((t0, swap_y(send, outer, ny)))
    out = elementwise(right_end, whole, value, got, table)
    last = pl.pallas_call(
        lambda *refs: end_bands(ny, outer, inner, *refs),
        out_shape=shape((ny * 2, low, width), BF),
        in_specs=[core_spec] + [vmem] * 4, out_specs=vmem, compiler_params=limit(8),
    )(core_ref, small, tile0, t0, back1)
    met, out = lax.optimization_barrier((lax.all_to_all(last, ("y", "c"), 0, 0), out))
    head = total(met)
    return lax.dynamic_update_slice(out, head, (0, 0))


def solution(mesh):
    rows, cols = mesh.devices.shape
    grid = Mesh(mesh.devices.reshape(grid_of(rows) + (cols,)), ("y", "z", "c", "x"))
    in_specs = (
        P(ROWS, "x"),
        P(None, None, ROWS),
        P(None, None, ROWS),
        P(ROWS),
        P(None, ROWS + ("x",), None),
        P(None, ROWS, None),
    )
    return jax.shard_map(
        shards, mesh=grid, in_specs=in_specs, out_specs=P(ROWS, "x"), check_vma=False)
```

```python
import jax
import jax.numpy as jnp
from jax import lax
from jax.experimental import pallas as pl
from jax.experimental.pallas import tpu as pltpu
from jax.sharding import Mesh, PartitionSpec as P

BF = jnp.bfloat16
F32 = jnp.float32
ROWS = ("y", "z", "c")
DOWN = (((0,), (0,)), ((), ()))


def limit(mib):
    return pltpu.CompilerParams(vmem_limit_bytes=mib * 2 ** 20)


def grid_of(rows):
    z = 8 if rows >= 128 else 4
    return rows // (2 * z), z, 2


def swap_y(v, bit, count):
    return lax.ppermute(v, "y", [(i, i ^ bit) for i in range(count)])


def swap_core(v):
    return lax.ppermute(v, "c", [(0, 1), (1, 0)])


def everyone(block, axes, count):
    return lax.all_to_all(jnp.broadcast_to(block[None], (count,) + block.shape), axes, 0, 0)


def two_parts(v):
    high = v.astype(BF)
    return high, (v - high.astype(F32)).astype(BF)


def total(v):
    return jnp.sum(v.astype(F32), axis=0)


def dot(a, b):
    return jnp.dot(a, b, preferred_element_type=F32)


def down(a, b):
    return lax.dot_general(a, b, DOWN, preferred_element_type=F32)


LO, LI, RO, RI, PIV = 0, 2, 4, 6, 8


def column(table, k):
    return table[:, k:k + 1]


def elementwise(body, outs, *args):
    size = sum(a.size * a.dtype.itemsize for a in args)
    return pl.pallas_call(
        body,
        out_shape=outs,
        compiler_params=limit(6),
        cost_estimate=pl.CostEstimate(flops=0, bytes_accessed=2 * size, transcendentals=0),
    )(*args)


def left_send(rhs, table, send):
    send[...] = (column(table, LO + 1) * rhs[...].astype(F32)).astype(BF)


def left_middle(rhs, got, table, value, send):
    v = column(table, LO) * rhs[...].astype(F32) + got[...].astype(F32)
    value[...] = column(table, LI) * v
    send[...] = (column(table, LI + 1) * v).astype(BF)


def right_middle(scaled, got, table, value, send):
    v = column(table, RI) * scaled[...] + column(table, RI + 1) * got[...].astype(F32)
    value[...] = column(table, RO) * v
    send[...] = v.astype(BF)


def right_end(value, got, table, out):
    out[...] = value[...] + column(table, RO + 1) * got[...].astype(F32)


def assemble(core, mine, other, solved):
    ny, half, _ = mine.shape
    for y in range(ny):
        for h in range(2):
            start = (2 * y + h) * half

            @pl.when(core[0] == h)
            def _():
                solved[start:start + half] = mine[y]

            @pl.when(core[0] != h)
            def _():
                solved[start:start + half] = other[y]


def first_update(core, panel, mine, other, value, got, base, solved):
    @pl.when(pl.program_id(0) == 0)
    def _():
        assemble(core, mine, other, solved)

    base[...] = value[...] + got[...].astype(F32) - dot(panel[...], solved[...])


def split_term(core, acc, mine, away):
    ny, half, width = mine.shape
    for y in range(ny):
        for h in range(2):
            start = (2 * y + h) * half
            block = acc[:, start:start + half].T

            @pl.when(core[0] == h)
            def _():
                mine[y] = block

            @pl.when(core[0] != h)
            def _():
                away[y] = block.astype(BF)


def middle(
        low, tile, core, panel, own, other, base, table, scaled, rounded, mine, away, acc, solved):
    step = pl.program_id(0)

    @pl.when(step == 0)
    def _():
        assemble(core, own, other, solved)

    v = (base[...] - dot(panel[...], solved[...])) / column(table, PIV)
    scaled[...] = v
    row = lax.broadcasted_iota(jnp.int32, v.shape, 0) + step * tile
    kept = jnp.where(row >= low, v, 0.0)
    rounded[...] = kept.astype(BF)
    add = dot(kept.T.astype(BF), panel[...])

    @pl.when(step == 0)
    def _():
        acc[...] = add

    @pl.when(step > 0)
    def _():
        acc[...] += add

    @pl.when(step == pl.num_programs(0) - 1)
    def _():
        split_term(core, acc, mine, away)


def first_term(core, panel, rounded, mine, away, acc):
    step = pl.program_id(0)
    add = dot(rounded[...].astype(F32).T.astype(BF), panel[...])

    @pl.when(step == 0)
    def _():
        acc[...] = add

    @pl.when(step > 0)
    def _():
        acc[...] += add

    @pl.when(step == pl.num_programs(0) - 1)
    def _():
        split_term(core, acc, mine, away)


def second_input(core, x1, mine_rows, other_rows, solved, spread, rows):
    ny, half, width = solved.shape
    rb = mine_rows.shape[0]
    first = jnp.where(core[0] == 0, 1.0, 0.0)

    @pl.when(core[0] == 0)
    def _():
        rows[:rb] = mine_rows[...]
        rows[rb:] = other_rows[...]

    @pl.when(core[0] != 0)
    def _():
        rows[:rb] = other_rows[...]
        rows[rb:] = mine_rows[...]

    v = first * x1[...]
    for y in range(ny):
        start = pl.multiple_of((2 * y + core[0]) * half, half)
        v = v - dot(rows[:, pl.ds(start, half)], solved[y])
    v = v.astype(BF)
    for y in range(ny):
        spread[y] = v


def cross_back(core, tile, target, cross, term, away, back, out):
    ny, half, _ = term.shape
    v = dot(tile[...], target[...])
    back[...] = v
    turned = v.T.astype(BF)
    for y in range(ny):
        start = pl.multiple_of((2 * y + core[0]) * half, half)
        share = dot(turned, cross[:, pl.ds(start, half)]).T
        out[y] = (term[y] + away[y].astype(F32) + share).astype(BF)


def end_bands(ny, outer, inner, core, coefs, tile, target, back1, last):
    n, rb = coefs.shape[:2]
    first = jnp.where(core[0] == 0, 1.0, 0.0)
    values = [dot(tile[...], target[...]), first * back1[...]]
    for b in range(2):
        v = [values[b][i * rb:(i + 1) * rb] for i in range(n)]
        for level, bit in ((RI, 2 * inner), (RO, 2 * outer)):
            k = 2 * level + b
            v = [coefs[i][:, k:k + 1] * v[i] + coefs[i][:, k + 2:k + 3] * v[i ^ bit]
                 for i in range(n)]
        for i in range(n):
            last[i, b * rb:(b + 1) * rb] = v[i].astype(BF)


def spread_sum(arrived, count, base=None, pivots=None):
    rb, width = arrived.shape[1:]

    def body(*refs):
        own, spread = refs[-2:]
        v = jnp.sum(refs[0][...].astype(F32), axis=0)
        if base is not None:
            v = refs[1][...] / refs[2][...] - v
        own[...] = v
        v = v.astype(BF)
        for i in range(count):
            spread[i] = v

    args = (arrived,) if base is None else (arrived, base, pivots)
    return pl.pallas_call(
        body,
        out_shape=(jax.ShapeDtypeStruct((rb, width), F32),
                   jax.ShapeDtypeStruct((count, rb, width), BF)),
        cost_estimate=pl.CostEstimate(
            flops=0, bytes_accessed=2 * arrived.size, transcendentals=0),
        compiler_params=limit(4),
    )(*args)


def start_bands(ny, outer, inner, coefs, arrived, part, x1):
    rb, width = arrived.shape[2:]
    n = 2 * ny

    def fly(b, i, level, v):
        bit = (outer if level == 0 else inner) * 2
        own = level * 4 + b
        j = i ^ bit
        a = coefs[i][:, own:own + 1] * v[i]
        return a + coefs[j][:, own + 2:own + 3] * v[j]

    both = []
    for b in range(2):
        raw = [arrived[i, 3 + b].astype(F32) for i in range(n)]
        first = [fly(b, i, 0, raw) for i in range(n)]
        both.append([fly(b, i, 1, first) for i in range(n)])
    tile = jnp.concatenate([arrived[i, 0] for i in range(n)], axis=0)
    x0 = jnp.concatenate(both[0], axis=0).astype(BF)
    part[...] = down(tile, x0).astype(BF)
    for i in range(n):
        x1[i] = both[1][i]


def shards(rhs, left, right, pivots, panels, inverse):
    ny, nz = lax.axis_size("y"), lax.axis_size("z")
    rb, band = inverse.shape[1], inverse.shape[2]
    rows, width = rhs.shape
    half = nz * rb
    low = 2 * rb
    core, y = lax.axis_index("c"), lax.axis_index("y")
    outer, inner = ny // 2, ny // 4
    chunk = ny * 2 * rb
    core_ref = core.astype(jnp.int32)[None]

    def reduce_yz(mine):
        return lax.all_to_all(mine.astype(BF).reshape(ny * nz, rb, width), ("y", "z"), 0, 0)

    def gather_yz(spread):
        return lax.all_to_all(spread, ("y", "z"), 0, 0).reshape(ny, half, width)

    gathered0 = lax.all_gather(panels[0], "x", axis=0, tiled=True)

    table = jnp.concatenate([left.reshape(4, rows), right.reshape(4, rows), pivots[None]], axis=0)
    table = jnp.pad(table, ((0, 7), (0, 0))).T

    few = table[:low].reshape(2, rb, 16).transpose(1, 2, 0).reshape(rb, 32)
    few = jnp.concatenate(two_parts(few), axis=1)
    few = jnp.pad(few, ((0, 0), (0, half - few.shape[1])))
    blocks = inverse.reshape(2, rb, ny, 2, half)
    wide0 = blocks[0].transpose(1, 2, 0, 3)[:, :, None]
    wide1 = jnp.broadcast_to(blocks[1].transpose(1, 2, 0, 3)[:, None], (ny, 2, 2, rb, half))
    shared = jnp.concatenate([rhs[:low].reshape(2, rb, half), few[None]], axis=0)
    shared = jnp.broadcast_to(shared[None, None], (ny, 2, 3, rb, half))
    message = jnp.concatenate([wide0, wide1, shared], axis=2).reshape(ny * 2, 6, rb, half)
    arrived = lax.all_to_all(message, ("y", "c"), 0, 0)

    to_owner = [(i, (i % nz) * 2 + i // nz) for i in range(2 * nz)]
    own_pivots = lax.ppermute(
        jnp.broadcast_to(table[:low, PIV:PIV + 1], (low, width)), ("z", "c"), to_owner)

    shape = jax.ShapeDtypeStruct
    whole, sent = shape((rows, width), F32), shape((rows, width), BF)
    send = elementwise(left_send, sent, rhs, table)
    arrived, own_pivots, send = lax.optimization_barrier((arrived, own_pivots, send))
    got = swap_y(send, outer, ny)

    small = arrived[:, 5].astype(F32)
    small = small[:, :, :32] + small[:, :, 32:64]
    tile0 = arrived[:, 0].reshape(chunk, half)
    tile1 = jnp.concatenate(
        [arrived[:, 1].reshape(chunk, half), arrived[:, 2].reshape(chunk, half)], axis=1)

    part, x1 = pl.pallas_call(
        lambda *refs: start_bands(ny, outer, inner, *refs),
        out_shape=(shape((half, width), BF), shape((ny * 2, rb, width), F32)),
        compiler_params=limit(8),
    )(small, arrived)
    x1 = lax.dynamic_slice_in_dim(x1, 2 * y, 2, 0).reshape(low, width)

    met = lax.all_to_all(part.reshape(nz, rb, width), "z", 0, 0)
    met, got = lax.optimization_barrier((met, got))
    own0, spread = spread_sum(met, ny * nz)
    spread, second = lax.optimization_barrier((spread, panels[1]))
    gathered1 = lax.all_gather(second, "x", axis=0, tiled=True)
    mine0 = gather_yz(spread)
    mine0, got = lax.optimization_barrier((mine0, got))
    value, send = elementwise(left_middle, (whole, sent), rhs, got, table)
    crossed = swap_y(send, inner, ny)

    core_spec = pl.BlockSpec(memory_space=pltpu.SMEM)
    vmem = pl.BlockSpec(memory_space=pltpu.VMEM)
    cross = gathered0[rb:low]
    spread = pl.pallas_call(
        second_input, out_shape=shape((ny, low, width), BF),
        in_specs=[core_spec] + [vmem] * 4, out_specs=vmem,
        scratch_shapes=[pltpu.VMEM((low, band), BF)], compiler_params=limit(6),
    )(core_ref, x1, cross, swap_core(cross), mine0)
    x1 = lax.all_to_all(spread, "y", 0, 0).reshape(chunk, width)
    other0 = swap_core(mine0)
    part = down(tile1, x1).astype(BF).reshape(2 * nz, rb, width)
    met = lax.all_to_all(part, ("c", "z"), 0, 0)
    met, other0, crossed = lax.optimization_barrier((met, other0, crossed))
    own1, spread = spread_sum(met, ny * nz)

    tile = rows // 3
    steps = rows // tile
    panel_spec = pl.BlockSpec((tile, band), lambda i: (i, 0))
    row_spec = pl.BlockSpec((tile, width), lambda i: (i, 0))
    table_spec = pl.BlockSpec((tile, 16), lambda i: (i, 0))
    half_spec = pl.BlockSpec((ny, half, width), lambda i: (0, 0, 0))
    params = limit(20)
    cost = pl.CostEstimate(
        flops=2 * rows * band * width, bytes_accessed=2 * rows * band, transcendentals=0)
    solved_ref = pltpu.VMEM((band, width), BF)
    base = pl.pallas_call(
        first_update, out_shape=whole, grid=(steps,),
        in_specs=[core_spec, panel_spec, half_spec, half_spec, row_spec, row_spec],
        out_specs=row_spec, scratch_shapes=[solved_ref],
        cost_estimate=cost,
    )(core_ref, gathered0, mine0, other0, value, crossed)

    mine1 = gather_yz(spread)
    mine1, base, cross, gathered1 = lax.optimization_barrier((mine1, base, cross, gathered1))
    cross = lax.all_gather(cross, ("y", "c"), axis=0, tiled=True)
    other1 = swap_core(mine1)
    halves = (shape((ny, half, width), F32), shape((ny, half, width), BF))
    scaled, rounded, term1, away1 = pl.pallas_call(
        lambda *refs: middle(low, tile, *refs),
        out_shape=(whole, sent) + halves, grid=(steps,),
        in_specs=[core_spec, panel_spec, half_spec, half_spec, row_spec, table_spec],
        out_specs=(row_spec, row_spec, half_spec, half_spec),
        scratch_shapes=[pltpu.VMEM((width, band), F32), solved_ref],
        cost_estimate=cost,
    )(core_ref, gathered1, mine1, other1, base, table)
    met = reduce_yz(term1 + swap_core(away1).astype(F32))

    term0, away0 = pl.pallas_call(
        first_term, out_shape=halves, grid=(steps,),
        in_specs=[core_spec, panel_spec, row_spec], out_specs=(half_spec, half_spec),
        scratch_shapes=[pltpu.VMEM((width, band), F32)],
        compiler_params=params, cost_estimate=cost,
    )(core_ref, gathered0, rounded)
    away0 = swap_core(away0)
    met, term0, away0 = lax.optimization_barrier((met, term0, away0))
    _, spread = spread_sum(met, 2 * nz, own1, own_pivots[rb:])

    got = swap_y(rounded, inner, ny)
    t1 = lax.all_to_all(spread, ("c", "z"), 0, 0).reshape(2 * half, width)
    t1, got, cross = lax.optimization_barrier((t1, got, cross))
    value, send = elementwise(right_middle, (whole, sent), scaled, got, table)
    back1, term0 = pl.pallas_call(
        cross_back, out_shape=(shape((chunk, width), F32), shape((ny, half, width), BF)),
        in_specs=[core_spec] + [vmem] * 5, out_specs=(vmem, vmem),
    )(core_ref, tile1, t1, cross, term0, away0)
    met = reduce_yz(term0)
    _, spread = spread_sum(met, nz, own0, own_pivots[:rb])
    t0 = lax.all_to_all(spread, "z", 0, 0).reshape(half, width)
    t0, got = lax.optimization_barrier((t0, swap_y(send, outer, ny)))
    out = elementwise(right_end, whole, value, got, table)
    last = pl.pallas_call(
        lambda *refs: end_bands(ny, outer, inner, *refs),
        out_shape=shape((ny * 2, low, width), BF),
        in_specs=[core_spec] + [vmem] * 4, out_specs=vmem, compiler_params=limit(8),
    )(core_ref, small, tile0, t0, back1)
    met, out = lax.optimization_barrier((lax.all_to_all(last, ("y", "c"), 0, 0), out))
    head = total(met)
    return lax.dynamic_update_slice(out, head, (0, 0))


def solution(mesh):
    rows, cols = mesh.devices.shape
    grid = Mesh(mesh.devices.reshape(grid_of(rows) + (cols,)), ("y", "z", "c", "x"))
    in_specs = (
        P(ROWS, "x"),
        P(None, None, ROWS),
        P(None, None, ROWS),
        P(ROWS),
        P(None, ROWS + ("x",), None),
        P(None, ROWS, None),
    )
    return jax.shard_map(
        shards, mesh=grid, in_specs=in_specs, out_specs=P(ROWS, "x"), check_vma=False)
```

```python
import jax
import jax.numpy as jnp
from jax import lax
from jax.experimental import pallas as pl
from jax.experimental.pallas import tpu as pltpu
from jax.sharding import Mesh, PartitionSpec as P

BF = jnp.bfloat16
F32 = jnp.float32
ROWS = ("y", "z", "c")
DOWN = (((0,), (0,)), ((), ()))


def limit(mib):
    return pltpu.CompilerParams(vmem_limit_bytes=mib * 2 ** 20)


def grid_of(rows):
    z = 8 if rows >= 128 else 4
    return rows // (2 * z), z, 2


def swap_y(v, bit, count):
    return lax.ppermute(v, "y", [(i, i ^ bit) for i in range(count)])


def swap_core(v):
    return lax.ppermute(v, "c", [(0, 1), (1, 0)])


def everyone(block, axes, count):
    return lax.all_to_all(jnp.broadcast_to(block[None], (count,) + block.shape), axes, 0, 0)


def two_parts(v):
    high = v.astype(BF)
    return high, (v - high.astype(F32)).astype(BF)


def total(v):
    return jnp.sum(v.astype(F32), axis=0)


def dot(a, b):
    return jnp.dot(a, b, preferred_element_type=F32)


def down(a, b):
    return lax.dot_general(a, b, DOWN, preferred_element_type=F32)


LO, LI, RO, RI, PIV = 0, 2, 4, 6, 8


def column(table, k):
    return table[:, k:k + 1]


def elementwise(body, outs, *args):
    size = sum(a.size * a.dtype.itemsize for a in args)
    return pl.pallas_call(
        body,
        out_shape=outs,
        compiler_params=limit(6),
        cost_estimate=pl.CostEstimate(flops=0, bytes_accessed=2 * size, transcendentals=0),
    )(*args)


def left_send(rhs, table, send):
    send[...] = (column(table, LO + 1) * rhs[...].astype(F32)).astype(BF)


def left_middle(rhs, got, table, value, send):
    v = column(table, LO) * rhs[...].astype(F32) + got[...].astype(F32)
    value[...] = column(table, LI) * v
    send[...] = (column(table, LI + 1) * v).astype(BF)


def right_middle(scaled, got, table, value, send):
    v = column(table, RI) * scaled[...] + column(table, RI + 1) * got[...].astype(F32)
    value[...] = column(table, RO) * v
    send[...] = v.astype(BF)


def right_end(value, got, table, out):
    out[...] = value[...] + column(table, RO + 1) * got[...].astype(F32)


def assemble(core, mine, other, solved):
    ny, half, _ = mine.shape
    for y in range(ny):
        for h in range(2):
            start = (2 * y + h) * half

            @pl.when(core[0] == h)
            def _():
                solved[start:start + half] = mine[y]

            @pl.when(core[0] != h)
            def _():
                solved[start:start + half] = other[y]


def first_update(core, panel, mine, other, value, got, base, solved):
    @pl.when(pl.program_id(0) == 0)
    def _():
        assemble(core, mine, other, solved)

    base[...] = value[...] + got[...].astype(F32) - dot(panel[...], solved[...])


def split_term(core, acc, mine, away):
    ny, half, width = mine.shape
    for y in range(ny):
        for h in range(2):
            start = (2 * y + h) * half
            block = acc[:, start:start + half].T

            @pl.when(core[0] == h)
            def _():
                mine[y] = block

            @pl.when(core[0] != h)
            def _():
                away[y] = block.astype(BF)


def middle(
        low, tile, core, panel, own, other, base, table, scaled, rounded, mine, away, acc, solved):
    step = pl.program_id(0)

    @pl.when(step == 0)
    def _():
        assemble(core, own, other, solved)

    v = (base[...] - dot(panel[...], solved[...])) / column(table, PIV)
    scaled[...] = v
    row = lax.broadcasted_iota(jnp.int32, v.shape, 0) + step * tile
    kept = jnp.where(row >= low, v, 0.0)
    rounded[...] = kept.astype(BF)
    add = dot(kept.T.astype(BF), panel[...])

    @pl.when(step == 0)
    def _():
        acc[...] = add

    @pl.when(step > 0)
    def _():
        acc[...] += add

    @pl.when(step == pl.num_programs(0) - 1)
    def _():
        split_term(core, acc, mine, away)


def first_term(core, panel, rounded, mine, away, acc):
    step = pl.program_id(0)
    add = dot(rounded[...].astype(F32).T.astype(BF), panel[...])

    @pl.when(step == 0)
    def _():
        acc[...] = add

    @pl.when(step > 0)
    def _():
        acc[...] += add

    @pl.when(step == pl.num_programs(0) - 1)
    def _():
        split_term(core, acc, mine, away)


def second_input(core, x1, mine_rows, other_rows, solved, spread, rows):
    ny, half, width = solved.shape
    rb = mine_rows.shape[0]
    first = jnp.where(core[0] == 0, 1.0, 0.0)

    @pl.when(core[0] == 0)
    def _():
        rows[:rb] = mine_rows[...]
        rows[rb:] = other_rows[...]

    @pl.when(core[0] != 0)
    def _():
        rows[:rb] = other_rows[...]
        rows[rb:] = mine_rows[...]

    v = first * x1[...]
    for y in range(ny):
        start = pl.multiple_of((2 * y + core[0]) * half, half)
        v = v - dot(rows[:, pl.ds(start, half)], solved[y])
    v = v.astype(BF)
    for y in range(ny):
        spread[y] = v


def cross_back(core, tile, target, cross, term, away, back, out):
    ny, half, _ = term.shape
    v = dot(tile[...], target[...])
    back[...] = v
    turned = v.T.astype(BF)
    for y in range(ny):
        start = pl.multiple_of((2 * y + core[0]) * half, half)
        share = dot(turned, cross[:, pl.ds(start, half)]).T
        out[y] = (term[y] + away[y].astype(F32) + share).astype(BF)


def end_bands(ny, outer, inner, core, coefs, tile, target, back1, last):
    n, rb = coefs.shape[:2]
    first = jnp.where(core[0] == 0, 1.0, 0.0)
    values = [dot(tile[...], target[...]), first * back1[...]]
    for b in range(2):
        v = [values[b][i * rb:(i + 1) * rb] for i in range(n)]
        for level, bit in ((RI, 2 * inner), (RO, 2 * outer)):
            k = 2 * level + b
            v = [coefs[i][:, k:k + 1] * v[i] + coefs[i][:, k + 2:k + 3] * v[i ^ bit]
                 for i in range(n)]
        for i in range(n):
            last[i, b * rb:(b + 1) * rb] = v[i].astype(BF)


def spread_sum(arrived, count, base=None, pivots=None):
    rb, width = arrived.shape[1:]

    def body(*refs):
        own, spread = refs[-2:]
        v = jnp.sum(refs[0][...].astype(F32), axis=0)
        if base is not None:
            v = refs[1][...] / refs[2][...] - v
        own[...] = v
        v = v.astype(BF)
        for i in range(count):
            spread[i] = v

    args = (arrived,) if base is None else (arrived, base, pivots)
    return pl.pallas_call(
        body,
        out_shape=(jax.ShapeDtypeStruct((rb, width), F32),
                   jax.ShapeDtypeStruct((count, rb, width), BF)),
        cost_estimate=pl.CostEstimate(
            flops=0, bytes_accessed=2 * arrived.size, transcendentals=0),
        compiler_params=limit(4),
    )(*args)


def start_bands(ny, outer, inner, coefs, arrived, part, x1):
    rb, width = arrived.shape[2:]
    n = 2 * ny

    def fly(b, i, level, v):
        bit = (outer if level == 0 else inner) * 2
        own = level * 4 + b
        j = i ^ bit
        a = coefs[i][:, own:own + 1] * v[i]
        return a + coefs[j][:, own + 2:own + 3] * v[j]

    both = []
    for b in range(2):
        raw = [arrived[i, 3 + b].astype(F32) for i in range(n)]
        first = [fly(b, i, 0, raw) for i in range(n)]
        both.append([fly(b, i, 1, first) for i in range(n)])
    tile = jnp.concatenate([arrived[i, 0] for i in range(n)], axis=0)
    x0 = jnp.concatenate(both[0], axis=0).astype(BF)
    part[...] = down(tile, x0).astype(BF)
    for i in range(n):
        x1[i] = both[1][i]


def shards(rhs, left, right, pivots, panels, inverse):
    ny, nz = lax.axis_size("y"), lax.axis_size("z")
    rb, band = inverse.shape[1], inverse.shape[2]
    rows, width = rhs.shape
    half = nz * rb
    low = 2 * rb
    core, y = lax.axis_index("c"), lax.axis_index("y")
    outer, inner = ny // 2, ny // 4
    chunk = ny * 2 * rb
    core_ref = core.astype(jnp.int32)[None]

    def reduce_yz(mine):
        return lax.all_to_all(mine.astype(BF).reshape(ny * nz, rb, width), ("y", "z"), 0, 0)

    def gather_yz(spread):
        return lax.all_to_all(spread, ("y", "z"), 0, 0).reshape(ny, half, width)

    gathered0 = lax.all_gather(panels[0], "x", axis=0, tiled=True)

    table = jnp.concatenate([left.reshape(4, rows), right.reshape(4, rows), pivots[None]], axis=0)
    table = jnp.pad(table, ((0, 7), (0, 0))).T

    few = table[:low].reshape(2, rb, 16).transpose(1, 2, 0).reshape(rb, 32)
    few = jnp.concatenate(two_parts(few), axis=1)
    few = jnp.pad(few, ((0, 0), (0, half - few.shape[1])))
    blocks = inverse.reshape(2, rb, ny, 2, half)
    wide0 = blocks[0].transpose(1, 2, 0, 3)[:, :, None]
    wide1 = jnp.broadcast_to(blocks[1].transpose(1, 2, 0, 3)[:, None], (ny, 2, 2, rb, half))
    shared = jnp.concatenate([rhs[:low].reshape(2, rb, half), few[None]], axis=0)
    shared = jnp.broadcast_to(shared[None, None], (ny, 2, 3, rb, half))
    message = jnp.concatenate([wide0, wide1, shared], axis=2).reshape(ny * 2, 6, rb, half)
    arrived = lax.all_to_all(message, ("y", "c"), 0, 0)

    to_owner = [(i, (i % nz) * 2 + i // nz) for i in range(2 * nz)]
    own_pivots = lax.ppermute(
        jnp.broadcast_to(table[:low, PIV:PIV + 1], (low, width)), ("z", "c"), to_owner)

    shape = jax.ShapeDtypeStruct
    whole, sent = shape((rows, width), F32), shape((rows, width), BF)
    send = elementwise(left_send, sent, rhs, table)
    arrived, own_pivots = lax.optimization_barrier((arrived, own_pivots))
    got = swap_y(send, outer, ny)

    small = arrived[:, 5].astype(F32)
    small = small[:, :, :32] + small[:, :, 32:64]
    tile0 = arrived[:, 0].reshape(chunk, half)
    tile1 = jnp.concatenate(
        [arrived[:, 1].reshape(chunk, half), arrived[:, 2].reshape(chunk, half)], axis=1)

    part, x1 = pl.pallas_call(
        lambda *refs: start_bands(ny, outer, inner, *refs),
        out_shape=(shape((half, width), BF), shape((ny * 2, rb, width), F32)),
        compiler_params=limit(8),
    )(small, arrived)
    x1 = lax.dynamic_slice_in_dim(x1, 2 * y, 2, 0).reshape(low, width)

    met = lax.all_to_all(part.reshape(nz, rb, width), "z", 0, 0)
    met, got = lax.optimization_barrier((met, got))
    own0, spread = spread_sum(met, ny * nz)
    spread, second = lax.optimization_barrier((spread, panels[1]))
    gathered1 = lax.all_gather(second, "x", axis=0, tiled=True)
    mine0 = gather_yz(spread)
    mine0, got = lax.optimization_barrier((mine0, got))
    value, send = elementwise(left_middle, (whole, sent), rhs, got, table)
    crossed = swap_y(send, inner, ny)

    core_spec = pl.BlockSpec(memory_space=pltpu.SMEM)
    vmem = pl.BlockSpec(memory_space=pltpu.VMEM)
    cross = gathered0[rb:low]
    spread = pl.pallas_call(
        second_input, out_shape=shape((ny, low, width), BF),
        in_specs=[core_spec] + [vmem] * 4, out_specs=vmem,
        scratch_shapes=[pltpu.VMEM((low, band), BF)], compiler_params=limit(6),
    )(core_ref, x1, cross, swap_core(cross), mine0)
    x1 = lax.all_to_all(spread, "y", 0, 0).reshape(chunk, width)
    other0 = swap_core(mine0)
    part = down(tile1, x1).astype(BF).reshape(2 * nz, rb, width)
    met = lax.all_to_all(part, ("c", "z"), 0, 0)
    met, other0, crossed = lax.optimization_barrier((met, other0, crossed))
    own1, spread = spread_sum(met, ny * nz)

    tile = rows // 3
    steps = rows // tile
    panel_spec = pl.BlockSpec((tile, band), lambda i: (i, 0))
    row_spec = pl.BlockSpec((tile, width), lambda i: (i, 0))
    table_spec = pl.BlockSpec((tile, 16), lambda i: (i, 0))
    half_spec = pl.BlockSpec((ny, half, width), lambda i: (0, 0, 0))
    params = limit(20)
    cost = pl.CostEstimate(
        flops=2 * rows * band * width, bytes_accessed=2 * rows * band, transcendentals=0)
    solved_ref = pltpu.VMEM((band, width), BF)
    base = pl.pallas_call(
        first_update, out_shape=whole, grid=(steps,),
        in_specs=[core_spec, panel_spec, half_spec, half_spec, row_spec, row_spec],
        out_specs=row_spec, scratch_shapes=[solved_ref],
        cost_estimate=cost,
    )(core_ref, gathered0, mine0, other0, value, crossed)

    mine1 = gather_yz(spread)
    mine1, base, cross, gathered1 = lax.optimization_barrier((mine1, base, cross, gathered1))
    cross = lax.all_gather(cross, ("y", "c"), axis=0, tiled=True)
    other1 = swap_core(mine1)
    halves = (shape((ny, half, width), F32), shape((ny, half, width), BF))
    scaled, rounded, term1, away1 = pl.pallas_call(
        lambda *refs: middle(low, tile, *refs),
        out_shape=(whole, sent) + halves, grid=(steps,),
        in_specs=[core_spec, panel_spec, half_spec, half_spec, row_spec, table_spec],
        out_specs=(row_spec, row_spec, half_spec, half_spec),
        scratch_shapes=[pltpu.VMEM((width, band), F32), solved_ref],
        cost_estimate=cost,
    )(core_ref, gathered1, mine1, other1, base, table)
    met = reduce_yz(term1 + swap_core(away1).astype(F32))

    term0, away0 = pl.pallas_call(
        first_term, out_shape=halves, grid=(steps,),
        in_specs=[core_spec, panel_spec, row_spec], out_specs=(half_spec, half_spec),
        scratch_shapes=[pltpu.VMEM((width, band), F32)],
        compiler_params=params, cost_estimate=cost,
    )(core_ref, gathered0, rounded)
    away0 = swap_core(away0)
    met, term0, away0 = lax.optimization_barrier((met, term0, away0))
    _, spread = spread_sum(met, 2 * nz, own1, own_pivots[rb:])

    got = swap_y(rounded, inner, ny)
    t1 = lax.all_to_all(spread, ("c", "z"), 0, 0).reshape(2 * half, width)
    t1, got, cross = lax.optimization_barrier((t1, got, cross))
    value, send = elementwise(right_middle, (whole, sent), scaled, got, table)
    back1, term0 = pl.pallas_call(
        cross_back, out_shape=(shape((chunk, width), F32), shape((ny, half, width), BF)),
        in_specs=[core_spec] + [vmem] * 5, out_specs=(vmem, vmem),
    )(core_ref, tile1, t1, cross, term0, away0)
    met = reduce_yz(term0)
    _, spread = spread_sum(met, nz, own0, own_pivots[:rb])
    t0 = lax.all_to_all(spread, "z", 0, 0).reshape(half, width)
    t0, got = lax.optimization_barrier((t0, swap_y(send, outer, ny)))
    out = elementwise(right_end, whole, value, got, table)
    last = pl.pallas_call(
        lambda *refs: end_bands(ny, outer, inner, *refs),
        out_shape=shape((ny * 2, low, width), BF),
        in_specs=[core_spec] + [vmem] * 4, out_specs=vmem, compiler_params=limit(8),
    )(core_ref, small, tile0, t0, back1)
    met, out = lax.optimization_barrier((lax.all_to_all(last, ("y", "c"), 0, 0), out))
    head = total(met)
    return lax.dynamic_update_slice(out, head, (0, 0))


def solution(mesh):
    rows, cols = mesh.devices.shape
    grid = Mesh(mesh.devices.reshape(grid_of(rows) + (cols,)), ("y", "z", "c", "x"))
    in_specs = (
        P(ROWS, "x"),
        P(None, None, ROWS),
        P(None, None, ROWS),
        P(ROWS),
        P(None, ROWS + ("x",), None),
        P(None, ROWS, None),
    )
    return jax.shard_map(
        shards, mesh=grid, in_specs=in_specs, out_specs=P(ROWS, "x"), check_vma=False)
```
